128 devices in a mesh: row: 8 (over x, y_lo), col: 16 (over y_hi, z, core).
Axes of the slice: x: 4, y: 4 (y_hi: 2, y_lo: 2; y = y_hi * 2 + y_lo), z: 4, core: 2. Of those that a mesh axis runs over, the one named last changes fastest.
Arguments:
- latent: bfloat16 [256, 512, 512], P('row', 'col'), may hold values from -12 to 12
- conv_scale: float32 [512], replicated, may hold values from 0.5 to 1.5
- conv_shift: float32 [512], replicated, may hold values from -3 to 3
- expand_weight: bfloat16 [512, 2048], replicated, may hold values from -0.25 to 0.25
- depth_kernel: float32 [9, 2048], replicated, may hold values from -2 to 2
- squeeze_down: bfloat16 [2048, 128], replicated, may hold values from -0.5 to 0.5
- squeeze_up: bfloat16 [128, 2048], replicated, may hold values from -0.5 to 0.5
- project_weight: bfloat16 [2048, 512], replicated, may hold values from -0.125 to 0.125
- block_gain: float32 [512], replicated, may hold values from 0.5 to 1.5
- block_projection: bfloat16 [512, 1536], replicated, may hold values from -0.25 to 0.25
- block_output: bfloat16 [512, 512], replicated, may hold values from -0.25 to 0.25
- block_table: float32 [16, 225], replicated, may hold values from -4 to 300
- first_gain: float32 [512], replicated, may hold values from 0.5 to 1.5
- first_expand: bfloat16 [512, 2048], replicated, may hold values from -0.25 to 0.25
- first_reduce: bfloat16 [2048, 512], replicated, may hold values from -0.125 to 0.125
- grid_gain: float32 [512], replicated, may hold values from 0.5 to 1.5
- grid_projection: bfloat16 [512, 1536], replicated, may hold values from -0.25 to 0.25
- grid_output: bfloat16 [512, 512], replicated, may hold values from -0.25 to 0.25
- grid_table: float32 [16, 225], replicated, may hold values from -4 to 300
- second_gain: float32 [512], replicated, may hold values from 0.5 to 1.5
- second_expand: bfloat16 [512, 2048], replicated, may hold values from -0.25 to 0.25
- second_reduce: bfloat16 [2048, 512], replicated, may hold values from -0.125 to 0.125
Outputs:
- nowcast_latent: bfloat16 [256, 512, 512], P('row', 'col')
The draws below stay inside these ranges and needn't reach their ends.
All inputs are finite; a program needn't handle non-finite values.
Results may differ from the reference program's by a relative error of at most 0.012.
Values may be sent and summed in bfloat16 or wider, within the bound.
No kernel may reach another device: no remote copies, remote signals or barrier semaphores. Data moves between devices by JAX's collectives and lax.ppermute only.
A program may use at most 128 MiB of HBM per device.

```python
import jax
import jax.numpy as jnp
from jax import lax

C = 512
HEADS = 16
E = 2048
FF = 2048
SQUEEZE = 128
WIN = 8
HEIGHT = 256
WIDTH = 512
N_ROW = 8
N_COL = 16


def draw_latent(key, part):
    key = jax.random.fold_in(key, 7301)
    row_key = jax.random.fold_in(key, 0)
    col_key = jax.random.fold_in(key, 1)
    main_key = jax.random.fold_in(key, 2)
    offset_key = jax.random.fold_in(key, 4)
    patch_key = jax.random.fold_in(key, 5)
    rising = 3.0 ** (jnp.arange(HEIGHT, dtype=jnp.float32) / max(HEIGHT - 1, 1))
    row_factor = rising * jnp.exp(jax.random.uniform(row_key, (HEIGHT,), jnp.float32, -0.35, 0.35))
    col_factor = jnp.exp(jax.random.uniform(col_key, (WIDTH,), jnp.float32, -0.35, 0.35))
    base = jnp.clip(jax.random.normal(main_key, (HEIGHT, WIDTH, C), jnp.float32), -4.0, 4.0)
    centre_key, across_key, tall_key, broad_key = jax.random.split(patch_key, 4)
    centre_row = jax.random.uniform(centre_key, (4,), jnp.float32, 0.0, 1.0)
    centre_col = jax.random.uniform(across_key, (4,), jnp.float32, 0.05, 0.95)
    half_row = jax.random.uniform(tall_key, (4,), jnp.float32, 0.2, 0.45)
    half_col = jax.random.uniform(broad_key, (4,), jnp.float32, 0.06, 0.12)
    row_spot = (jnp.arange(HEIGHT, dtype=jnp.float32) + 0.5) / HEIGHT
    col_spot = (jnp.arange(WIDTH, dtype=jnp.float32) + 0.5) / WIDTH
    storm = jnp.zeros((HEIGHT, WIDTH), jnp.float32)
    for patch in range(4):
        row_inside = jax.nn.sigmoid((half_row[patch] - jnp.abs(row_spot - centre_row[patch])) / 0.02)
        col_inside = jax.nn.sigmoid((half_col[patch] - jnp.abs(col_spot - centre_col[patch])) / 0.01)
        storm = storm + row_inside[:, None] * col_inside[None, :]
    storm = jnp.clip(storm, 0.0, 1.0)
    channel_offset = jax.random.uniform(offset_key, (C,), jnp.float32, -2.5, 2.5)
    shaped = base * row_factor[:, None, None] * col_factor[None, :, None] / 1.7 * (1.0 + 0.5 * storm[:, :, None])
    shaped = shaped + (2.0 * storm - 1.0)[:, :, None] * channel_offset
    return jnp.clip(shaped, -12.0, 12.0).astype(jnp.bfloat16)


def relative_table(key, salt):
    key = jax.random.fold_in(key, salt)
    base_key = jax.random.fold_in(key, 0)
    spots = (2 * WIN - 1) ** 2
    base = jnp.clip(jax.random.normal(base_key, (HEADS, spots), jnp.float32), -4.0, 4.0)
    return base.astype(jnp.float32)


def draw_block_table(key, part):
    return relative_table(key, 8101)


def draw_grid_table(key, part):
    return relative_table(key, 8209)


def noise(rng, shape, deviation, bound, kind=jnp.bfloat16):
    return jnp.clip(deviation * jax.random.normal(rng, shape, jnp.float32), -bound, bound).astype(kind)


def setup_inputs(seed: int = 0) -> dict:
    streams_of = jax.random.split(jax.random.key(seed), 23)
    return {
        "latent": draw_latent(jax.random.fold_in(streams_of[22], 71), 0),
        "conv_scale": jnp.clip(1.0 + 0.1 * jax.random.normal(streams_of[1], (C,), jnp.float32), 0.5, 1.5),
        "conv_shift": noise(streams_of[2], (C,), 0.5, 3.0, jnp.float32),
        "expand_weight": noise(streams_of[3], (C, E), C ** -0.5, 0.25),
        "depth_kernel": noise(streams_of[4], (9, E), 9 ** -0.5, 2.0, jnp.float32),
        "squeeze_down": noise(streams_of[5], (E, SQUEEZE), SQUEEZE ** -0.5, 0.5),
        "squeeze_up": noise(streams_of[6], (SQUEEZE, E), SQUEEZE ** -0.5, 0.5),
        "project_weight": noise(streams_of[7], (E, C), E ** -0.5, 0.125),
        "block_gain": jnp.clip(1.0 + 0.1 * jax.random.normal(streams_of[8], (C,), jnp.float32), 0.5, 1.5),
        "block_projection": noise(streams_of[9], (C, 3 * C), C ** -0.5, 0.25),
        "block_output": noise(streams_of[10], (C, C), C ** -0.5, 0.25),
        "block_table": draw_block_table(jax.random.fold_in(streams_of[22], 71), 0),
        "first_gain": jnp.clip(1.0 + 0.1 * jax.random.normal(streams_of[12], (C,), jnp.float32), 0.5, 1.5),
        "first_expand": noise(streams_of[13], (C, FF), C ** -0.5, 0.25),
        "first_reduce": noise(streams_of[14], (FF, C), FF ** -0.5, 0.125),
        "grid_gain": jnp.clip(1.0 + 0.1 * jax.random.normal(streams_of[15], (C,), jnp.float32), 0.5, 1.5),
        "grid_projection": noise(streams_of[16], (C, 3 * C), C ** -0.5, 0.25),
        "grid_output": noise(streams_of[17], (C, C), C ** -0.5, 0.25),
        "grid_table": draw_grid_table(jax.random.fold_in(streams_of[22], 71), 0),
        "second_gain": jnp.clip(1.0 + 0.1 * jax.random.normal(streams_of[19], (C,), jnp.float32), 0.5, 1.5),
        "second_expand": noise(streams_of[20], (C, FF), C ** -0.5, 0.25),
        "second_reduce": noise(streams_of[21], (FF, C), FF ** -0.5, 0.125),
    }


def layer_norm_apply(values, norm_gain):
    widened = values.astype(jnp.float32)
    center = widened - lax.optimization_barrier(jnp.mean(widened, axis=-1, keepdims=True))
    spread = lax.optimization_barrier(jnp.mean(center * center, axis=-1, keepdims=True))
    return (center * lax.rsqrt(spread + 1e-05) * norm_gain).astype(jnp.bfloat16)

def position_bias(offset_bias_lookup):
    position = jnp.arange(WIN * WIN)
    down_pos = position // WIN
    across = position % WIN
    relative = (down_pos[:, None] - down_pos[None, :] + WIN - 1) * (2 * WIN - 1) + (across[:, None] - across[None, :] + WIN - 1)
    return offset_bias_lookup[:, relative]

def attend(triple, pos_bias):
    window_count, tokens, three_width = triple.shape
    feature_width = three_width // 3
    head_count = pos_bias.shape[0]
    head_size = feature_width // head_count
    queries = triple[..., :feature_width].reshape(window_count, tokens, head_count, head_size).astype(jnp.float32)
    key_row_list = triple[..., feature_width:2 * feature_width].reshape(window_count, tokens, head_count, head_size).astype(jnp.float32)
    values = triple[..., 2 * feature_width:].reshape(window_count, tokens, head_count, head_size).astype(jnp.float32)
    scores = jnp.einsum('nqhd,nkhd->nhqk', queries, key_row_list) * head_size ** (-0.5) + pos_bias[None]
    row_max = lax.optimization_barrier(jnp.max(scores, axis=-1, keepdims=True))
    weight_tensors = jnp.exp(scores - row_max)
    attention_weight_map = (weight_tensors / lax.optimization_barrier(jnp.sum(weight_tensors, axis=-1, keepdims=True))).astype(jnp.bfloat16)
    mixed = jnp.einsum('nhqk,nkhd->nqhd', attention_weight_map.astype(jnp.float32), values)
    return mixed.astype(jnp.bfloat16).reshape(window_count, tokens, feature_width)

def attention_sublayer(windows, norm_gain, in_weight, out_weight, pos_bias):
    normed = layer_norm_apply(windows, norm_gain)
    triple = jnp.dot(normed, in_weight, preferred_element_type=jnp.float32).astype(jnp.bfloat16)
    per_device = triple.shape[0] // (N_ROW * N_COL)
    grouped = triple.reshape(N_ROW * N_COL, per_device, WIN * WIN, triple.shape[-1])
    mixed = lax.map(lambda blocked: attend(blocked, pos_bias), grouped)
    mixed = mixed.reshape(windows.shape[0], WIN * WIN, -1)
    return (windows.astype(jnp.float32) + jnp.dot(mixed, out_weight, preferred_element_type=jnp.float32)).astype(jnp.bfloat16)

def feed_forward(values, norm_gain, in_weight, out_weight):
    normed = layer_norm_apply(values, norm_gain)
    hidden = jax.nn.gelu(jnp.dot(normed, in_weight, preferred_element_type=jnp.float32), approximate=True).astype(jnp.bfloat16)
    return (values.astype(jnp.float32) + jnp.dot(hidden, out_weight, preferred_element_type=jnp.float32)).astype(jnp.bfloat16)

def block_windows(field):
    feats = field.shape[-1]
    return field.reshape(HEIGHT // WIN, WIN, WIDTH // WIN, WIN, feats).transpose(0, 2, 1, 3, 4).reshape(-1, WIN * WIN, feats)

def block_field(windows):
    feats = windows.shape[-1]
    return windows.reshape(HEIGHT // WIN, WIDTH // WIN, WIN, WIN, feats).transpose(0, 2, 1, 3, 4).reshape(HEIGHT, WIDTH, feats)

def grid_windows(field):
    feats = field.shape[-1]
    return field.reshape(WIN, HEIGHT // WIN, WIN, WIDTH // WIN, feats).transpose(1, 3, 0, 2, 4).reshape(-1, WIN * WIN, feats)

def grid_field(windows):
    feats = windows.shape[-1]
    return windows.reshape(HEIGHT // WIN, WIDTH // WIN, WIN, WIN, feats).transpose(2, 0, 3, 1, 4).reshape(HEIGHT, WIDTH, feats)

def squeeze_gate(pooled, squeeze_down, squeeze_up):
    reduced = jax.nn.silu(jnp.dot(pooled[None, :], squeeze_down.astype(jnp.float32), precision=lax.Precision.HIGHEST))
    return jax.nn.sigmoid(jnp.dot(reduced, squeeze_up.astype(jnp.float32), precision=lax.Precision.HIGHEST))[0]

def reference(latent, conv_scale, conv_shift, expand_weight, depth_kernel, squeeze_down, squeeze_up, project_weight, block_gain, block_projection, block_output, block_table, first_gain, first_expand, first_reduce, grid_gain, grid_projection, grid_output, grid_table, second_gain, second_expand, second_reduce):
    conv_in = (latent.astype(jnp.float32) * conv_scale + conv_shift).astype(jnp.bfloat16)
    expanded = jax.nn.gelu(jnp.dot(conv_in, expand_weight, preferred_element_type=jnp.float32), approximate=True).astype(jnp.bfloat16)
    padded = jnp.pad(expanded, ((1, 1), (1, 1), (0, 0)))
    summed = jnp.zeros(expanded.shape, jnp.float32)
    for offset in range(9):
        down_step = offset // 3
        side_step = offset % 3
        summed = summed + padded[down_step:down_step + HEIGHT, side_step:side_step + WIDTH].astype(jnp.float32) * depth_kernel[offset]
    depthwise = jax.nn.gelu(summed, approximate=True)
    pooled = lax.optimization_barrier(jnp.sum(depthwise, axis=(0, 1))) / (HEIGHT * WIDTH)
    excite = squeeze_gate(pooled, squeeze_down, squeeze_up)
    gated = (depthwise * excite).astype(jnp.bfloat16)
    conv_out = (latent.astype(jnp.float32) + jnp.dot(gated, project_weight, preferred_element_type=jnp.float32)).astype(jnp.bfloat16)
    section = block_field(attention_sublayer(block_windows(conv_out), block_gain, block_projection, block_output, position_bias(block_table)))
    section = feed_forward(section, first_gain, first_expand, first_reduce)
    section = grid_field(attention_sublayer(grid_windows(section), grid_gain, grid_projection, grid_output, position_bias(grid_table)))
    return feed_forward(section, second_gain, second_expand, second_reduce)
```

```python
import jax
import jax.numpy as jnp
from jax import lax
from jax.experimental import pallas as pl
from jax.experimental.pallas import tpu as pltpu
from jax.sharding import Mesh, PartitionSpec as P

BF = jnp.bfloat16
F32 = jnp.float32


def norm(xf, g):
    center = xf - jnp.mean(xf, axis=-1, keepdims=True)
    spread = jnp.mean(center * center, axis=-1, keepdims=True)
    return (center * lax.rsqrt(spread + 1e-05) * g).astype(BF)


def gelu(v):
    half = 0.5 * v
    return half + half * jnp.tanh(v * (0.7978845608028654 + 0.035677408136300125 * (v * v)))


def dot(a, b):
    return jnp.dot(a, b, preferred_element_type=F32)


def dot_nt(a, b):
    return lax.dot_general(a, b, (((1,), (1,)), ((), ())), preferred_element_type=F32)


def dot_tn(a, b):
    return lax.dot_general(a, b, (((0,), (0,)), ((), ())), preferred_element_type=F32)


def attn_ff(x, g1, pk, pqvt, o, bias, g2, u, w, mixt, kbuf, qvt, ff_block=512):
    m = x.shape[0]
    xf = x.astype(F32)
    n = norm(xf, g1[...])
    kbuf[...] = dot(n, pk[...]).astype(BF)
    qvt[...] = dot_nt(pqvt[...], n).astype(BF)
    low = lax.broadcasted_iota(jnp.int32, (64, 128), 1) < 64
    zero = jnp.zeros((32, 128), BF)

    def pair(p, carry):
        lanes = pl.ds(pl.multiple_of(p * 128, 128), 128)
        for g in range(4):
            keys = kbuf[lanes, 128 * g:128 * g + 128]
            q = [qvt[128 * g + 32 * h:128 * g + 32 * h + 32, lanes] for h in range(4)]
            qbd = jnp.concatenate(
                [jnp.concatenate([q[h] if j == h else zero for j in range(4)], axis=0) for h in range(4)],
                axis=1)
            s4 = dot(keys, qbd)
            for h in range(4):
                head = 4 * g + h
                s = s4[:, 128 * h:128 * h + 128]
                s = jnp.where(low, s[:64], s[64:]) * (32 ** -0.5) + bias[head]
                e = jnp.exp(s - jnp.max(s, axis=0, keepdims=True))
                r = 1.0 / jnp.sum(e, axis=0, keepdims=True)
                pbd = jnp.concatenate(
                    [jnp.where(low, e, 0.0).astype(BF), jnp.where(low, 0.0, e).astype(BF)], axis=0)
                vt = qvt[512 + 32 * head:544 + 32 * head, lanes]
                mixt[32 * head:32 * head + 32, lanes] = (dot(vt, pbd) * r).astype(BF)
        return carry

    lax.fori_loop(0, m // 128, pair, 0)
    y = (xf + dot_tn(mixt[...], o[...])).astype(BF)
    yf = y.astype(F32)
    n2 = norm(yf, g2[...])
    acc = yf
    for j in range(u.shape[1] // ff_block):
        cols = slice(j * ff_block, (j + 1) * ff_block)
        hidden = gelu(dot(n2, u[:, cols])).astype(BF)
        acc = acc + dot(hidden, w[cols, :])
    return acc.astype(BF)


def section_body(x, g1, pk, pqvt, o, bias, g2, u, w, out, mixt, kbuf, qvt):
    out[...] = attn_ff(x[...], g1, pk, pqvt, o, bias, g2, u, w, mixt, kbuf, qvt)


def whole(shape):
    return pl.BlockSpec(shape, lambda i: (0,) * len(shape))


def section_call(x, g1, pk, pqvt, o, bias, g2, u, w, m=256):
    cells, feats = x.shape
    args = (g1.reshape(1, -1), pk, pqvt, o, bias, g2.reshape(1, -1), u, w)
    return pl.pallas_call(
        section_body,
        grid=(cells // m,),
        in_specs=[pl.BlockSpec((m, feats), lambda i: (i, 0))] + [whole(a.shape) for a in args],
        out_specs=pl.BlockSpec((m, feats), lambda i: (i, 0)),
        out_shape=jax.ShapeDtypeStruct((cells, feats), BF),
        scratch_shapes=[pltpu.VMEM((feats, m), BF), pltpu.VMEM((m, feats), BF), pltpu.VMEM((2 * feats, m), BF)],
        compiler_params=pltpu.CompilerParams(vmem_limit_bytes=48 * 2**20),
    )(x, *args)


def bias_table(table):
    t = table.reshape(-1, 15, 15)
    rows = jnp.stack([t[:, 7 - q:15 - q] for q in range(8)], axis=1)
    both = jnp.stack([rows[..., 7 - q:15 - q] for q in range(8)], axis=2)
    out = both.reshape(-1, 64, 64)
    return jnp.concatenate([out, out], axis=-1)


def extended(cells, sides, width):
    for axis, dim, count in sides:
        ends = count - 1
        head = lax.slice_in_dim(cells, 0, width, axis=dim)
        tail = lax.slice_in_dim(cells, cells.shape[dim] - width, cells.shape[dim], axis=dim)
        cells = jnp.concatenate(
            [
                lax.ppermute(tail, axis, [(i, i + 1) for i in range(ends)]),
                cells,
                lax.ppermute(head, axis, [(i + 1, i) for i in range(ends)]),
            ],
            axis=dim,
        )
    return cells


def squeeze_gate(pooled, squeeze_down, squeeze_up):
    reduced = jax.nn.silu(
        jnp.dot(pooled[None, :], squeeze_down.astype(F32), precision=lax.Precision.HIGHEST)
    )
    return jax.nn.sigmoid(
        jnp.dot(reduced, squeeze_up.astype(F32), precision=lax.Precision.HIGHEST)
    )[0]


def channel_total(sums):
    sums = sums + lax.ppermute(sums, "core", [(0, 1), (1, 0)])
    width = sums.shape[0]
    copies = jnp.broadcast_to(sums.reshape(1, width // 128, 128), (64, width // 128, 128))
    copies = lax.all_to_all(copies, ("row", "ch"), 0, 0, tiled=True)
    return copies.sum(0).reshape(width)


def swap(windows):
    return lax.all_to_all(
        windows.reshape(16, 64, -1), ("row", "ch"), split_axis=1, concat_axis=1, tiled=True
    ).reshape(1024, -1)


def per_device(
    latent, conv_scale, conv_shift, expand_weight, depth_kernel, squeeze_down, squeeze_up, project_weight,
    block_gain, block_projection, block_output, block_table, first_gain, first_expand, first_reduce,
    grid_gain, grid_projection, grid_output, grid_table, second_gain, second_expand, second_reduce,
):
    row_count, col_count, channels = latent.shape
    conv_in = (latent.astype(F32) * conv_scale + conv_shift).astype(BF)
    expanded = jax.nn.gelu(dot(conv_in, expand_weight), approximate=True).astype(BF)
    padded = extended(expanded, (("row", 0, 8), (("ch", "core"), 1, 16)), 1)
    summed = jnp.zeros((row_count, col_count, padded.shape[-1]), F32)
    for offset in range(9):
        down_step = offset // 3
        side_step = offset % 3
        summed = (
            summed
            + padded[down_step : down_step + row_count, side_step : side_step + col_count].astype(F32)
            * depth_kernel[offset]
        )
    depthwise = jax.nn.gelu(summed, approximate=True)
    channel_sums = channel_total(jnp.sum(depthwise, axis=(0, 1)))
    excite = squeeze_gate(channel_sums / (256 * 512), squeeze_down, squeeze_up)
    gated = (depthwise * excite).astype(BF)
    conv_out = (latent.astype(F32) + dot(gated, project_weight)).astype(BF)
    windows = conv_out.reshape(4, 8, 4, 8, channels).transpose(0, 2, 1, 3, 4).reshape(1024, channels)

    def split(projection):
        keys = projection[:, channels : 2 * channels]
        others = jnp.concatenate([projection[:, :channels], projection[:, 2 * channels :]], axis=1).T
        return keys, others

    windows = section_call(
        windows, block_gain, *split(block_projection), block_output, bias_table(block_table),
        first_gain, first_expand, first_reduce,
    )
    windows = swap(windows)
    windows = section_call(
        windows, grid_gain, *split(grid_projection), grid_output, bias_table(grid_table),
        second_gain, second_expand, second_reduce,
    )
    windows = swap(windows)
    return windows.reshape(4, 4, 8, 8, channels).transpose(0, 2, 1, 3, 4).reshape(row_count, col_count, channels)


def solution(mesh):
    wide = Mesh(mesh.devices.reshape(8, 8, 2), ("row", "ch", "core"))
    field = P("row", ("ch", "core"), None)
    return jax.shard_map(
        per_device, mesh=wide, in_specs=(field,) + (P(),) * 21, out_specs=field, check_vma=False
    )
```

```python
import jax
import jax.numpy as jnp
from jax import lax
from jax.experimental import pallas as pl
from jax.experimental.pallas import tpu as pltpu
from jax.sharding import Mesh, PartitionSpec as P

BF = jnp.bfloat16
F32 = jnp.float32
CELLS = 1024
HALO = 160


def norm(xf, g):
    center = xf - jnp.mean(xf, axis=-1, keepdims=True)
    spread = jnp.mean(center * center, axis=-1, keepdims=True)
    return (center * lax.rsqrt(spread + 1e-05) * g).astype(BF)


def gelu(v):
    half = 0.5 * v
    return half + half * jnp.tanh(v * (0.7978845608028654 + 0.035677408136300125 * (v * v)))


def dot(a, b):
    return jnp.dot(a, b, preferred_element_type=F32)


def dot_nt(a, b):
    return lax.dot_general(a, b, (((1,), (1,)), ((), ())), preferred_element_type=F32)


def dot_tn(a, b):
    return lax.dot_general(a, b, (((0,), (0,)), ((), ())), preferred_element_type=F32)


def swapped(rows, cols):
    size = rows * cols
    to = lax.broadcasted_iota(jnp.int32, (size, size), 0)
    come = lax.broadcasted_iota(jnp.int32, (size, size), 1)
    return (come == (to % rows) * cols + to // rows).astype(F32).astype(BF)


def pieces(v):
    high = v.astype(BF)
    rest = v - high.astype(F32)
    mid = rest.astype(BF)
    return high, mid, (rest - mid.astype(F32)).astype(BF)


def whole(shape):
    return pl.BlockSpec(shape, lambda i: (0,) * len(shape))


def bias_body(block_tab, grid_tab, block_out, grid_out, turned):
    lane = lax.broadcasted_iota(jnp.int32, (256, 128), 1) % 64
    spot = lax.broadcasted_iota(jnp.int32, (256, 128), 0)
    for tab, out, column_major in ((block_tab, block_out, True), (grid_tab, grid_out, False)):
        slow, fast = lane // 8, lane % 8
        row, col = (fast, slow) if column_major else (slow, fast)
        pick = (spot == (row + 7) * 15 + col + 7).astype(F32).astype(BF)
        slow_step, fast_step = (1, 15) if column_major else (15, 1)
        for head in range(16):
            base = jnp.broadcast_to(tab[head:head + 1, :], (8, 256))
            for q in range(8):
                turned[64 * head + 8 * q:64 * head + 8 * q + 8, :] = pltpu.roll(
                    base, slow_step * q, 1, stride=fast_step, stride_axis=0)
        high, mid, low = pieces(turned[...])
        out[...] = (dot(high, pick) + dot(mid, pick) + dot(low, pick)).reshape(16, 64, 128)


def bias_call(block_table, grid_table):
    pad = lambda t: jnp.pad(t, ((0, 0), (0, 256 - t.shape[1])))
    shape = jax.ShapeDtypeStruct((16, 64, 128), F32)
    return pl.pallas_call(
        bias_body,
        grid=(1,),
        in_specs=[whole((16, 256))] * 2,
        out_specs=[whole((16, 64, 128))] * 2,
        out_shape=[shape, shape],
        scratch_shapes=[pltpu.VMEM((1024, 256), F32)],
        compiler_params=pltpu.CompilerParams(vmem_limit_bytes=16 * 2**20),
    )(pad(block_table), pad(grid_table))


def conv_body(flags, latent, above, below, left, right, scale, shift, weight, taps,
              ordered, depthwise, sums, conv_in, field):
    lanes = weight.shape[1]
    blocks = lanes // 128

    @pl.when(pl.program_id(0) == 0)
    def _():
        turn = swapped(8, 32)
        for i in range(4):
            part = dot(turn, latent[8 * i:8 * i + 8].reshape(256, 512))
            ordered[256 * i:256 * i + 256, :] = part.astype(BF)
            conv_in[256 * i:256 * i + 256, :] = (part * scale[...] + shift[...]).astype(BF)
        start = CELLS
        for edge in (above, below, left, right):
            size = edge.shape[0]
            conv_in[start:start + size, :] = (edge[...].astype(F32) * scale[...] + shift[...]).astype(BF)
            start += size

    halo = gelu(dot(conv_in[CELLS:CELLS + HALO, :], weight[...])).astype(BF).astype(F32)
    place = lax.broadcasted_iota(jnp.int32, (48, 1), 0)
    corner = jnp.where(place == 32, flags[0], jnp.where(place == 33, flags[1], 1.0))
    top, bottom = halo[0:32] * flags[0], halo[32:64] * flags[1]
    west, east = halo[64:112] * (corner * flags[2]), halo[112:160] * (corner * flags[3])
    for b in range(blocks):
        cut = slice(128 * b, 128 * b + 128)
        field[b, pl.ds(48 + 7, 32, stride=48), :] = top[:, cut]
        field[b, pl.ds(48 + 40, 32, stride=48), :] = bottom[:, cut]
        for side, at in ((west, 0), (east, 33 * 48)):
            field[b, at + 8:at + 40, :] = side[0:32, cut]
            field[b, at + 7:at + 8, :] = side[32:33, cut]
            field[b, at + 40:at + 41, :] = side[33:34, cut]

    def expand(i, carry):
        rows = pl.ds(pl.multiple_of(i * 256, 256), 256)
        res = gelu(dot(conv_in[rows, :], weight[...])).astype(BF).astype(F32)
        for b in range(blocks):
            for c in range(32):
                field[b, pl.ds(pl.multiple_of(48 * (c + 1) + 8 + 8 * i, 8), 8), :] = (
                    res[8 * c:8 * c + 8, 128 * b:128 * b + 128])
        return carry

    lax.fori_loop(0, 4, expand, 0)

    for b in range(blocks):
        cut = slice(128 * b, 128 * b + 128)
        k = [jnp.broadcast_to(taps[t:t + 1, cut], (8, 128)) for t in range(9)]

        def stencil(i, total):
            def partial(c):
                at = 48 * c + 8 + 8 * i
                up = field[b, pl.ds(at - 1, 8), :]
                mid = field[b, pl.ds(pl.multiple_of(at, 8), 8), :]
                down = field[b, pl.ds(at + 1, 8), :]
                return [k[t] * up + k[3 + t] * mid + k[6 + t] * down for t in range(3)]

            before = partial(0)
            now = partial(1)
            held = None
            for c in range(32):
                after = partial(c + 2)
                value = gelu(before[0] + now[1] + after[2])
                total = total + value
                before, now = now, after
                if c % 2 == 0:
                    held = value
                else:
                    rows = pl.ds(pl.multiple_of(256 * i + 8 * (c - 1), 16), 16)
                    depthwise[rows, cut] = jnp.concatenate([held, value], axis=0).astype(BF)
            return total

        total = lax.fori_loop(0, 4, stencil, jnp.zeros((8, 128), F32))
        sums[:, cut] = jnp.broadcast_to(jnp.sum(total, axis=0, keepdims=True), (8, 128))


def conv_call(flags, latent, above, below, left, right, scale, shift, weight, taps, lanes=512):
    channels, wide = weight.shape
    one = lambda v: v.reshape(1, -1)
    edges = [whole(e.shape) for e in (above, below, left, right)]
    return pl.pallas_call(
        conv_body,
        grid=(wide // lanes,),
        in_specs=[pl.BlockSpec(memory_space=pltpu.SMEM), whole(latent.shape)] + edges + [
            whole((1, channels)), whole((1, channels)),
            pl.BlockSpec((channels, lanes), lambda i: (0, i)),
            pl.BlockSpec((9, lanes), lambda i: (0, i)),
        ],
        out_specs=[
            whole((CELLS, channels)),
            pl.BlockSpec((CELLS, lanes), lambda i: (0, i)),
            pl.BlockSpec((8, lanes), lambda i: (0, i)),
        ],
        out_shape=[
            jax.ShapeDtypeStruct((CELLS, channels), BF),
            jax.ShapeDtypeStruct((CELLS, wide), BF),
            jax.ShapeDtypeStruct((8, wide), F32),
        ],
        scratch_shapes=[
            pltpu.VMEM((CELLS + HALO, channels), BF),
            pltpu.VMEM((lanes // 128, 34 * 48, 128), F32),
        ],
        compiler_params=pltpu.CompilerParams(vmem_limit_bytes=40 * 2**20),
    )(flags, latent, above, below, left, right, one(scale), one(shift), weight, taps)


def attn_ff(x, g1, pk, pqvt, o, bias, g2, u, w, mixt, kbuf, qvt, ff_block=512):
    m = x.shape[0]
    xf = x.astype(F32)
    n = norm(xf, g1[...])
    kbuf[...] = dot(n, pk[...]).astype(BF)
    qvt[...] = dot_nt(pqvt[...], n).astype(BF)
    low = lax.broadcasted_iota(jnp.int32, (64, 128), 1) < 64
    zero = jnp.zeros((32, 128), BF)

    def pair(p, carry):
        lanes = pl.ds(pl.multiple_of(p * 128, 128), 128)
        for g in range(4):
            keys = kbuf[lanes, 128 * g:128 * g + 128]
            q = [qvt[128 * g + 32 * h:128 * g + 32 * h + 32, lanes] for h in range(4)]
            qbd = jnp.concatenate(
                [jnp.concatenate([q[h] if j == h else zero for j in range(4)], axis=0) for h in range(4)],
                axis=1)
            s4 = dot(keys, qbd)
            for h in range(4):
                head = 4 * g + h
                s = s4[:, 128 * h:128 * h + 128]
                s = jnp.where(low, s[:64], s[64:]) * (32 ** -0.5) + bias[head]
                e = jnp.exp(s - jnp.max(s, axis=0, keepdims=True))
                r = 1.0 / jnp.sum(e, axis=0, keepdims=True)
                pbd = jnp.concatenate(
                    [jnp.where(low, e, 0.0).astype(BF), jnp.where(low, 0.0, e).astype(BF)], axis=0)
                vt = qvt[512 + 32 * head:544 + 32 * head, lanes]
                mixt[32 * head:32 * head + 32, lanes] = (dot(vt, pbd) * r).astype(BF)
        return carry

    lax.fori_loop(0, m // 128, pair, 0)
    y = (xf + dot_tn(mixt[...], o[...])).astype(BF)
    yf = y.astype(F32)
    n2 = norm(yf, g2[...])
    acc = yf
    for j in range(u.shape[1] // ff_block):
        cols = slice(j * ff_block, (j + 1) * ff_block)
        hidden = gelu(dot(n2, u[:, cols])).astype(BF)
        acc = acc + dot(hidden, w[cols, :])
    return acc.astype(BF)


def section_body(x, g1, pk, pqvt, o, bias, g2, u, w, out, mixt, kbuf, qvt):
    out[...] = attn_ff(x[...], g1, pk, pqvt, o, bias, g2, u, w, mixt, kbuf, qvt)


def gated_body(copies, down, up, depthwise, ordered, project, g1, pk, pqvt, o, bias, g2, u, w,
               out, mixt, kbuf, qvt, excite):
    @pl.when(pl.program_id(0) == 0)
    def _():
        pooled = jnp.sum(copies[...], axis=0) * (1.0 / (256 * 512))
        parts = pieces(pooled)
        reduced = jnp.zeros((1, down.shape[1]), F32)
        for b in range(pooled.shape[0]):
            for part in parts:
                row = jnp.broadcast_to(part[b:b + 1, :].astype(F32), (16, 128)).astype(BF)
                reduced = reduced + dot(row, down[128 * b:128 * b + 128, :])[0:1]
        reduced = reduced / (1.0 + jnp.exp(-reduced))
        raised = jnp.zeros((1, up.shape[1]), F32)
        for part in pieces(reduced):
            row = jnp.broadcast_to(part.astype(F32), (16, 128)).astype(BF)
            raised = raised + dot(row, up[...])[0:1]
        excite[...] = 1.0 / (1.0 + jnp.exp(-raised))

    acc = ordered[...].astype(F32)
    for j in range(4):
        cols = slice(512 * j, 512 * j + 512)
        gated = (depthwise[:, cols].astype(F32) * excite[:, cols]).astype(BF)
        acc = acc + dot(gated, project[cols, :])
    out[...] = attn_ff(acc.astype(BF), g1, pk, pqvt, o, bias, g2, u, w, mixt, kbuf, qvt)


def scratch(m, feats):
    return [pltpu.VMEM((feats, m), BF), pltpu.VMEM((m, feats), BF), pltpu.VMEM((2 * feats, m), BF)]


def section_call(x, g1, pk, pqvt, o, bias, g2, u, w, m=256):
    cells, feats = x.shape
    args = (g1.reshape(1, -1), pk, pqvt, o, bias, g2.reshape(1, -1), u, w)
    return pl.pallas_call(
        section_body,
        grid=(cells // m,),
        in_specs=[pl.BlockSpec((m, feats), lambda i: (i, 0))] + [whole(a.shape) for a in args],
        out_specs=pl.BlockSpec((m, feats), lambda i: (i, 0)),
        out_shape=jax.ShapeDtypeStruct((cells, feats), BF),
        scratch_shapes=scratch(m, feats),
        compiler_params=pltpu.CompilerParams(vmem_limit_bytes=40 * 2**20),
    )(x, *args)


def gated_call(copies, down, up, depthwise, ordered, project, g1, pk, pqvt, o, bias, g2, u, w, m=256):
    cells, feats = ordered.shape
    args = (project, g1.reshape(1, -1), pk, pqvt, o, bias, g2.reshape(1, -1), u, w)
    return pl.pallas_call(
        gated_body,
        grid=(cells // m,),
        in_specs=[whole(copies.shape), whole(down.shape), whole(up.shape),
                  pl.BlockSpec((m, depthwise.shape[1]), lambda i: (i, 0)),
                  pl.BlockSpec((m, feats), lambda i: (i, 0))] + [whole(a.shape) for a in args],
        out_specs=pl.BlockSpec((m, feats), lambda i: (i, 0)),
        out_shape=jax.ShapeDtypeStruct((cells, feats), BF),
        scratch_shapes=scratch(m, feats) + [pltpu.VMEM((1, depthwise.shape[1]), F32)],
        compiler_params=pltpu.CompilerParams(vmem_limit_bytes=44 * 2**20),
    )(copies, down, up, depthwise, ordered, *args)


def step(cells, axis, count, forward):
    pairs = [(i, i + 1) if forward else (i + 1, i) for i in range(count - 1)]
    return lax.ppermute(cells, axis, pairs)


def channel_copies(sums):
    sums = sums + lax.ppermute(sums, "core", [(0, 1), (1, 0)])
    width = sums.shape[0]
    copies = jnp.broadcast_to(sums.reshape(1, width // 128, 128), (64, width // 128, 128))
    return lax.all_to_all(copies, ("row", "ch"), 0, 0, tiled=True)


def swap(windows):
    return lax.all_to_all(
        windows.reshape(16, 64, -1), ("row", "ch"), split_axis=1, concat_axis=1, tiled=True
    ).reshape(1024, -1)


def per_device(
    latent, conv_scale, conv_shift, expand_weight, depth_kernel, squeeze_down, squeeze_up, project_weight,
    block_gain, block_projection, block_output, block_table, first_gain, first_expand, first_reduce,
    grid_gain, grid_projection, grid_output, grid_table, second_gain, second_expand, second_reduce,
):
    row_count, col_count, channels = latent.shape
    cols = ("ch", "core")
    above = step(latent[-1], "row", 8, True)
    below = step(latent[0], "row", 8, False)
    fill = jnp.zeros((14, channels), BF)
    left = step(jnp.concatenate([latent[:, -1], above[-1:], below[-1:], fill]), cols, 16, True)
    right = step(jnp.concatenate([latent[:, 0], above[:1], below[:1], fill]), cols, 16, False)
    row, col = lax.axis_index("row"), lax.axis_index(cols)
    flags = jnp.stack([row > 0, row < 7, col > 0, col < 15]).astype(F32)
    ordered, depthwise, sums = conv_call(
        flags, latent, above, below, left, right, conv_scale, conv_shift, expand_weight, depth_kernel
    )
    copies = channel_copies(sums[0])

    def split(projection):
        keys = projection[:, channels : 2 * channels]
        others = jnp.concatenate([projection[:, :channels], projection[:, 2 * channels :]], axis=1).T
        return keys, others

    block_bias, grid_bias = bias_call(block_table, grid_table)
    windows = gated_call(
        copies, squeeze_down, squeeze_up, depthwise, ordered, project_weight,
        block_gain, *split(block_projection), block_output, block_bias,
        first_gain, first_expand, first_reduce,
    )
    windows = swap(windows)
    windows = section_call(
        windows, grid_gain, *split(grid_projection), grid_output, grid_bias,
        second_gain, second_expand, second_reduce,
    )
    windows = swap(windows)
    return windows.reshape(4, 32, 8, channels).transpose(0, 2, 1, 3).reshape(row_count, col_count, channels)


def solution(mesh):
    wide = Mesh(mesh.devices.reshape(8, 8, 2), ("row", "ch", "core"))
    field = P("row", ("ch", "core"), None)
    return jax.shard_map(
        per_device, mesh=wide, in_specs=(field,) + (P(),) * 21, out_specs=field, check_vma=False
    )
```

```python
import jax
import jax.numpy as jnp
from jax import lax
from jax.experimental import pallas as pl
from jax.experimental.pallas import tpu as pltpu
from jax.sharding import Mesh, PartitionSpec as P

BF = jnp.bfloat16
F32 = jnp.float32
CELLS = 1024
HALO = 160


def norm(xf, g):
    center = xf - jnp.mean(xf, axis=-1, keepdims=True)
    spread = jnp.mean(center * center, axis=-1, keepdims=True)
    return (center * lax.rsqrt(spread + 1e-05) * g).astype(BF)


def gelu(v):
    half = 0.5 * v
    return half + half * jnp.tanh(v * (0.7978845608028654 + 0.035677408136300125 * (v * v)))


def dot(a, b):
    return jnp.dot(a, b, preferred_element_type=F32)


def dot_nt(a, b):
    return lax.dot_general(a, b, (((1,), (1,)), ((), ())), preferred_element_type=F32)


def dot_tn(a, b):
    return lax.dot_general(a, b, (((0,), (0,)), ((), ())), preferred_element_type=F32)


def swapped(rows, cols):
    size = rows * cols
    to = lax.broadcasted_iota(jnp.int32, (size, size), 0)
    come = lax.broadcasted_iota(jnp.int32, (size, size), 1)
    return (come == (to % rows) * cols + to // rows).astype(F32).astype(BF)


def pieces(v):
    high = v.astype(BF)
    rest = v - high.astype(F32)
    mid = rest.astype(BF)
    return high, mid, (rest - mid.astype(F32)).astype(BF)


def whole(shape):
    return pl.BlockSpec(shape, lambda i: (0,) * len(shape))


def bias_body(block_tab, grid_tab, block_out, grid_out, turned):
    lane = lax.broadcasted_iota(jnp.int32, (256, 128), 1) % 64
    spot = lax.broadcasted_iota(jnp.int32, (256, 128), 0)
    for tab, out, column_major in ((block_tab, block_out, True), (grid_tab, grid_out, False)):
        slow, fast = lane // 8, lane % 8
        row, col = (fast, slow) if column_major else (slow, fast)
        pick = (spot == (row + 7) * 15 + col + 7).astype(F32).astype(BF)
        slow_step, fast_step = (1, 15) if column_major else (15, 1)
        for head in range(16):
            base = jnp.broadcast_to(tab[head:head + 1, :], (8, 256))
            for q in range(8):
                turned[64 * head + 8 * q:64 * head + 8 * q + 8, :] = pltpu.roll(
                    base, slow_step * q, 1, stride=fast_step, stride_axis=0)
        high, mid, low = pieces(turned[...])
        out[...] = (dot(high, pick) + dot(mid, pick) + dot(low, pick)).reshape(16, 64, 128)


def bias_call(block_table, grid_table):
    pad = lambda t: jnp.pad(t, ((0, 0), (0, 256 - t.shape[1])))
    shape = jax.ShapeDtypeStruct((16, 64, 128), F32)
    return pl.pallas_call(
        bias_body,
        grid=(1,),
        in_specs=[whole((16, 256))] * 2,
        out_specs=[whole((16, 64, 128))] * 2,
        out_shape=[shape, shape],
        scratch_shapes=[pltpu.VMEM((1024, 256), F32)],
        compiler_params=pltpu.CompilerParams(vmem_limit_bytes=16 * 2**20),
    )(pad(block_table), pad(grid_table))


def conv_body(flags, latent, above, below, left, right, scale, shift, weight, taps,
              ordered, depthwise, sums, conv_in, field, totals):
    lanes = weight.shape[1]
    blocks = lanes // 128

    @pl.when(pl.program_id(0) == 0)
    def _():
        turn = swapped(8, 32)
        for i in range(4):
            part = dot(turn, latent[8 * i:8 * i + 8].reshape(256, 512))
            ordered[256 * i:256 * i + 256, :] = part.astype(BF)
            conv_in[256 * i:256 * i + 256, :] = (part * scale[...] + shift[...]).astype(BF)
        start = CELLS
        for edge in (above, below, left, right):
            size = edge.shape[0]
            conv_in[start:start + size, :] = (edge[...].astype(F32) * scale[...] + shift[...]).astype(BF)
            start += size

    halo = gelu(dot(conv_in[CELLS:CELLS + HALO, :], weight[...])).astype(BF).astype(F32)
    place = lax.broadcasted_iota(jnp.int32, (48, 1), 0)
    corner = jnp.where(place == 32, flags[0], jnp.where(place == 33, flags[1], 1.0))
    top, bottom = halo[0:32] * flags[0], halo[32:64] * flags[1]
    west, east = halo[64:112] * (corner * flags[2]), halo[112:160] * (corner * flags[3])
    for b in range(blocks):
        cut = slice(128 * b, 128 * b + 128)
        field[b, pl.ds(48 + 7, 32, stride=48), :] = top[:, cut]
        field[b, pl.ds(48 + 40, 32, stride=48), :] = bottom[:, cut]
        for side, at in ((west, 0), (east, 33 * 48)):
            field[b, at + 8:at + 40, :] = side[0:32, cut]
            field[b, at + 7:at + 8, :] = side[32:33, cut]
            field[b, at + 40:at + 41, :] = side[33:34, cut]

    def expand(i, carry):
        rows = pl.ds(pl.multiple_of(i * 256, 256), 256)
        res = gelu(dot(conv_in[rows, :], weight[...])).astype(BF).astype(F32)
        for b in range(blocks):
            for c in range(32):
                field[b, pl.ds(pl.multiple_of(48 * (c + 1) + 8 + 8 * i, 8), 8), :] = (
                    res[8 * c:8 * c + 8, 128 * b:128 * b + 128])
        return carry

    lax.fori_loop(0, 4, expand, 0)

    for b in range(blocks):
        cut = slice(128 * b, 128 * b + 128)
        k = [jnp.broadcast_to(taps[t:t + 1, cut], (8, 128)) for t in range(9)]

        def stencil(i, total):
            def partial(c):
                at = 48 * c + 8 + 8 * i
                up = field[b, pl.ds(at - 1, 8), :]
                mid = field[b, pl.ds(pl.multiple_of(at, 8), 8), :]
                down = field[b, pl.ds(at + 1, 8), :]
                return [k[t] * up + k[3 + t] * mid + k[6 + t] * down for t in range(3)]

            before = partial(0)
            now = partial(1)
            held = None
            for c in range(32):
                after = partial(c + 2)
                value = gelu(before[0] + now[1] + after[2])
                total = total + value
                before, now = now, after
                if c % 2 == 0:
                    held = value
                else:
                    rows = pl.ds(pl.multiple_of(256 * i + 8 * (c - 1), 16), 16)
                    depthwise[rows, cut] = jnp.concatenate([held, value], axis=0).astype(BF)
            return total

        total = lax.fori_loop(0, 4, stencil, jnp.zeros((8, 128), F32))
        totals[pl.ds(blocks * pl.program_id(0) + b, 1), :] = jnp.sum(total, axis=0, keepdims=True)

    @pl.when(pl.program_id(0) == pl.num_programs(0) - 1)
    def _():
        sums[...] = jnp.broadcast_to(totals[...].astype(BF)[None], sums.shape)


def conv_call(flags, latent, above, below, left, right, scale, shift, weight, taps, lanes=512):
    channels, wide = weight.shape
    one = lambda v: v.reshape(1, -1)
    edges = [whole(e.shape) for e in (above, below, left, right)]
    return pl.pallas_call(
        conv_body,
        grid=(wide // lanes,),
        in_specs=[pl.BlockSpec(memory_space=pltpu.SMEM), whole(latent.shape)] + edges + [
            whole((1, channels)), whole((1, channels)),
            pl.BlockSpec((channels, lanes), lambda i: (0, i)),
            pl.BlockSpec((9, lanes), lambda i: (0, i)),
        ],
        out_specs=[
            whole((CELLS, channels)),
            pl.BlockSpec((CELLS, lanes), lambda i: (0, i)),
            whole((128, wide // 128, 128)),
        ],
        out_shape=[
            jax.ShapeDtypeStruct((CELLS, channels), BF),
            jax.ShapeDtypeStruct((CELLS, wide), BF),
            jax.ShapeDtypeStruct((128, wide // 128, 128), BF),
        ],
        scratch_shapes=[
            pltpu.VMEM((CELLS + HALO, channels), BF),
            pltpu.VMEM((lanes // 128, 34 * 48, 128), F32),
            pltpu.VMEM((wide // 128, 128), F32),
        ],
        compiler_params=pltpu.CompilerParams(vmem_limit_bytes=60 * 2**20),
    )(flags, latent, above, below, left, right, one(scale), one(shift), weight, taps)


class Fetch:
    def __init__(self, sources, places, sems):
        self.copies = [pltpu.make_async_copy(s, p, sems.at[k]) for k, (s, p) in enumerate(zip(sources, places))]

    def start(self):
        for copy in self.copies:
            copy.start()

    def wait(self, *which):
        for k in which:
            self.copies[k].wait()


def attn_ff(x, wait, g1, p, pqvt, o, bias, g2, u, w, mixt, kbuf, qvt, ff_block=512):
    m, feats = x.shape
    xf = x.astype(F32)
    n = norm(xf, g1[...])
    wait(0, 1)
    kbuf[...] = dot(n, p[:, feats:2 * feats]).astype(BF)
    qvt[...] = dot_nt(pqvt[...], n).astype(BF)
    low = lax.broadcasted_iota(jnp.int32, (64, 128), 1) < 64
    zero = jnp.zeros((32, 128), BF)
    wait(2, 3)

    def pair(t, carry):
        lanes = pl.ds(pl.multiple_of(t * 128, 128), 128)
        for g in range(4):
            keys = kbuf[lanes, 128 * g:128 * g + 128]
            q = [qvt[128 * g + 32 * h:128 * g + 32 * h + 32, lanes] for h in range(4)]
            qbd = jnp.concatenate(
                [jnp.concatenate([q[h] if j == h else zero for j in range(4)], axis=0) for h in range(4)],
                axis=1)
            s4 = dot(keys, qbd)
            for h in range(4):
                head = 4 * g + h
                s = s4[:, 128 * h:128 * h + 128]
                s = jnp.where(low, s[:64], s[64:]) * (32 ** -0.5) + bias[head]
                e = jnp.exp(s - jnp.max(s, axis=0, keepdims=True))
                r = 1.0 / jnp.sum(e, axis=0, keepdims=True)
                pbd = jnp.concatenate(
                    [jnp.where(low, e, 0.0).astype(BF), jnp.where(low, 0.0, e).astype(BF)], axis=0)
                vt = qvt[512 + 32 * head:544 + 32 * head, lanes]
                mixt[32 * head:32 * head + 32, lanes] = (dot(vt, pbd) * r).astype(BF)
        return carry

    lax.fori_loop(0, m // 128, pair, 0, unroll=4)
    y = (xf + dot_tn(mixt[...], o[...])).astype(BF)
    yf = y.astype(F32)
    n2 = norm(yf, g2[...])
    acc = yf
    wait(4, 5)
    for j in range(u.shape[1] // ff_block):
        cols = slice(j * ff_block, (j + 1) * ff_block)
        hidden = gelu(dot(n2, u[:, cols])).astype(BF)
        acc = acc + dot(hidden, w[cols, :])
    return acc.astype(BF)


def turn_out(sec, out):
    def one(q, carry):
        for b in range(4):
            out[q, :, 128 * b:128 * b + 128] = sec[b, pl.ds(q, 16, stride=64), :].astype(BF)
        return carry

    lax.fori_loop(0, 64, one, 0, unroll=4)


def turn_in(x, sec):
    def one(q, carry):
        for b in range(4):
            sec[b, pl.ds(q, 16, stride=64), :] = x[q, :, 128 * b:128 * b + 128].astype(F32)
        return carry

    lax.fori_loop(0, 64, one, 0, unroll=4)


def section_body(x, g1, g2, p_h, pqvt_h, o_h, bias_h, u_h, w_h, out,
                 p, pqvt, o, bias, u, w, mixt, kbuf, qvt, sec, sems):
    fetch = Fetch((p_h, pqvt_h, o_h, bias_h, u_h, w_h), (p, pqvt, o, bias, u, w), sems)
    fetch.start()
    turn_in(x, sec)
    m = kbuf.shape[0]

    def chunk(i, carry):
        def wait(*which):
            @pl.when(i == 0)
            def _():
                fetch.wait(*which)

        rows = pl.ds(pl.multiple_of(i * m, m), m)
        cells = jnp.concatenate([sec[b, rows, :] for b in range(4)], axis=1).astype(BF)
        res = attn_ff(cells, wait, g1, p, pqvt, o, bias, g2, u, w, mixt, kbuf, qvt).astype(F32)
        for b in range(4):
            sec[b, rows, :] = res[:, 128 * b:128 * b + 128]
        return carry

    lax.fori_loop(0, CELLS // m, chunk, 0)
    turn_out(sec, out)


def gated_body(copies, g1, g2, down_h, up_h, project_h, ordered_h, depthwise_h,
               p_h, pqvt_h, o_h, bias_h, u_h, w_h, out,
               down, up, project, ordered, depthwise, p, pqvt, o, bias, u, w,
               mixt, kbuf, qvt, sec, excite, sems):
    fetch = Fetch(
        (down_h, up_h, project_h, ordered_h, depthwise_h, p_h, pqvt_h, o_h, bias_h, u_h, w_h),
        (down, up, project, ordered, depthwise, p, pqvt, o, bias, u, w), sems)
    fetch.start()
    pooled = jnp.sum(copies[...].astype(F32), axis=0) * (1.0 / (256 * 512))
    parts = pieces(pooled)
    reduced = jnp.zeros((1, down.shape[1]), F32)
    fetch.wait(0, 1)
    for b in range(pooled.shape[0]):
        row = jnp.concatenate([part[b:b + 1, :].astype(F32) for part in parts] + [jnp.zeros((13, 128), F32)], axis=0)
        reduced = reduced + jnp.sum(dot(row.astype(BF), down[128 * b:128 * b + 128, :]), axis=0, keepdims=True)
    reduced = reduced / (1.0 + jnp.exp(-reduced))
    row = jnp.concatenate([part.astype(F32) for part in pieces(reduced)] + [jnp.zeros((13, 128), F32)], axis=0)
    raised = jnp.sum(dot(row.astype(BF), up[...]), axis=0, keepdims=True)
    excite[...] = 1.0 / (1.0 + jnp.exp(-raised))
    m = kbuf.shape[0]
    fetch.wait(2, 3, 4)

    def chunk(i, carry):
        def wait(*which):
            @pl.when(i == 0)
            def _():
                fetch.wait(*[5 + k for k in which])

        rows = pl.ds(pl.multiple_of(i * m, m), m)
        acc = ordered[rows, :].astype(F32)
        for j in range(4):
            cols = slice(512 * j, 512 * j + 512)
            gated = (depthwise[rows, cols].astype(F32) * excite[:, cols]).astype(BF)
            acc = acc + dot(gated, project[cols, :])
        res = attn_ff(acc.astype(BF), wait, g1, p, pqvt, o, bias, g2, u, w, mixt, kbuf, qvt).astype(F32)
        for b in range(4):
            sec[b, rows, :] = res[:, 128 * b:128 * b + 128]
        return carry

    lax.fori_loop(0, CELLS // m, chunk, 0)
    turn_out(sec, out)


HELD = pl.BlockSpec(memory_space=pltpu.HBM)


def common_scratch(feats, m):
    return [pltpu.VMEM((feats, m), BF), pltpu.VMEM((m, feats), BF), pltpu.VMEM((2 * feats, m), BF),
            pltpu.VMEM((4, CELLS, 128), F32)]


def section_call(x, g1, g2, p, pqvt, o, bias, u, w, m=512):
    feats = x.shape[-1]
    held = (p, pqvt, o, bias, u, w)
    return pl.pallas_call(
        section_body,
        grid=(1,),
        in_specs=[whole(x.shape)] + [whole((1, feats))] * 2 + [HELD] * len(held),
        out_specs=whole((64, 16, feats)),
        out_shape=jax.ShapeDtypeStruct((64, 16, feats), BF),
        scratch_shapes=[pltpu.VMEM(a.shape, a.dtype) for a in held] + common_scratch(feats, m)
        + [pltpu.SemaphoreType.DMA((len(held),))],
        compiler_params=pltpu.CompilerParams(vmem_limit_bytes=60 * 2**20),
    )(x, g1.reshape(1, -1), g2.reshape(1, -1), *held)


def gated_call(copies, g1, g2, down, up, project, ordered, depthwise, p, pqvt, o, bias, u, w, m=512):
    feats = ordered.shape[-1]
    held = (down, up, project, ordered, depthwise, p, pqvt, o, bias, u, w)
    return pl.pallas_call(
        gated_body,
        grid=(1,),
        in_specs=[whole(copies.shape)] + [whole((1, feats))] * 2 + [HELD] * len(held),
        out_specs=whole((64, 16, feats)),
        out_shape=jax.ShapeDtypeStruct((64, 16, feats), BF),
        scratch_shapes=[pltpu.VMEM(a.shape, a.dtype) for a in held] + common_scratch(feats, m)
        + [pltpu.VMEM((1, depthwise.shape[1]), F32), pltpu.SemaphoreType.DMA((len(held),))],
        compiler_params=pltpu.CompilerParams(vmem_limit_bytes=60 * 2**20),
    )(copies, g1.reshape(1, -1), g2.reshape(1, -1), *held)


def step(cells, axis, count, forward):
    pairs = [(i, i + 1) if forward else (i + 1, i) for i in range(count - 1)]
    return lax.ppermute(cells, axis, pairs)


def per_device(
    latent, conv_scale, conv_shift, expand_weight, depth_kernel, squeeze_down, squeeze_up, project_weight,
    block_gain, block_projection, block_output, block_table, first_gain, first_expand, first_reduce,
    grid_gain, grid_projection, grid_output, grid_table, second_gain, second_expand, second_reduce,
):
    row_count, col_count, channels = latent.shape
    cols = ("ch", "core")
    above = step(latent[-1], "row", 8, True)
    below = step(latent[0], "row", 8, False)
    fill = jnp.zeros((14, channels), BF)
    left = step(jnp.concatenate([latent[:, -1], above[-1:], below[-1:], fill]), cols, 16, True)
    right = step(jnp.concatenate([latent[:, 0], above[:1], below[:1], fill]), cols, 16, False)
    row, col = lax.axis_index("row"), lax.axis_index(cols)
    flags = jnp.stack([row > 0, row < 7, col > 0, col < 15]).astype(F32)
    ordered, depthwise, copies = conv_call(
        flags, latent, above, below, left, right, conv_scale, conv_shift, expand_weight, depth_kernel
    )
    copies = lax.all_to_all(copies, ("row", "ch", "core"), 0, 0, tiled=True)

    def outer(projection):
        return jnp.concatenate([projection[:, :channels], projection[:, 2 * channels :]], axis=1).T

    def swap(windows):
        return lax.all_to_all(windows, ("row", "ch"), 0, 0, tiled=True)

    block_bias, grid_bias = bias_call(block_table, grid_table)
    windows = gated_call(
        copies, block_gain, first_gain, squeeze_down, squeeze_up, project_weight, ordered, depthwise,
        block_projection, outer(block_projection), block_output, block_bias, first_expand, first_reduce,
    )
    windows = section_call(
        swap(windows), grid_gain, second_gain,
        grid_projection, outer(grid_projection), grid_output, grid_bias, second_expand, second_reduce,
    )
    windows = swap(windows).reshape(8, 8, 4, 4, channels)
    return windows.transpose(2, 1, 3, 0, 4).reshape(row_count, col_count, channels)


def solution(mesh):
    wide = Mesh(mesh.devices.reshape(8, 8, 2), ("row", "ch", "core"))
    field = P("row", ("ch", "core"), None)
    return jax.shard_map(
        per_device, mesh=wide, in_specs=(field,) + (P(),) * 21, out_specs=field, check_vma=False
    )
```

```python
import jax
import jax.numpy as jnp
from jax import lax
from jax.experimental import pallas as pl
from jax.experimental.pallas import tpu as pltpu
from jax.sharding import Mesh, PartitionSpec as P

BF = jnp.bfloat16
F32 = jnp.float32
CELLS = 1024
HALO = 160


def norm(xf, g):
    center = xf - jnp.mean(xf, axis=-1, keepdims=True)
    spread = jnp.mean(center * center, axis=-1, keepdims=True)
    return (center * lax.rsqrt(spread + 1e-05) * g).astype(BF)


def gelu(v):
    v = v.astype(BF)
    half = v * 0.5
    return half + half * jnp.tanh(v * (v * v * 0.035677408136300125 + 0.7978845608028654))


def dot(a, b):
    return jnp.dot(a, b, preferred_element_type=F32)


def dot_nt(a, b):
    return lax.dot_general(a, b, (((1,), (1,)), ((), ())), preferred_element_type=F32)


def dot_tn(a, b):
    return lax.dot_general(a, b, (((0,), (0,)), ((), ())), preferred_element_type=F32)


def swapped(rows, cols):
    size = rows * cols
    to = lax.broadcasted_iota(jnp.int32, (size, size), 0)
    come = lax.broadcasted_iota(jnp.int32, (size, size), 1)
    return (come == (to % rows) * cols + to // rows).astype(F32).astype(BF)


def pieces(v):
    high = v.astype(BF)
    rest = v - high.astype(F32)
    mid = rest.astype(BF)
    return high, mid, (rest - mid.astype(F32)).astype(BF)


def whole(shape):
    return pl.BlockSpec(shape, lambda i: (0,) * len(shape))


def bias_body(block_tab, grid_tab, block_out, grid_out, turned):
    lane = lax.broadcasted_iota(jnp.int32, (256, 128), 1) % 64
    spot = lax.broadcasted_iota(jnp.int32, (256, 128), 0)
    for tab, out, column_major in ((block_tab, block_out, True), (grid_tab, grid_out, False)):
        slow, fast = lane // 8, lane % 8
        row, col = (fast, slow) if column_major else (slow, fast)
        pick = (spot == (row + 7) * 15 + col + 7).astype(F32).astype(BF)
        slow_step, fast_step = (1, 15) if column_major else (15, 1)
        for head in range(16):
            base = jnp.broadcast_to(tab[head:head + 1, :], (8, 256))
            for q in range(8):
                turned[64 * head + 8 * q:64 * head + 8 * q + 8, :] = pltpu.roll(
                    base, slow_step * q, 1, stride=fast_step, stride_axis=0)
        high, mid, low = pieces(turned[...])
        out[...] = (dot(high, pick) + dot(mid, pick) + dot(low, pick)).reshape(16, 64, 128)


def bias_call(block_table, grid_table):
    pad = lambda t: jnp.pad(t, ((0, 0), (0, 256 - t.shape[1])))
    shape = jax.ShapeDtypeStruct((16, 64, 128), F32)
    return pl.pallas_call(
        bias_body,
        grid=(1,),
        in_specs=[whole((16, 256))] * 2,
        out_specs=[whole((16, 64, 128))] * 2,
        out_shape=[shape, shape],
        scratch_shapes=[pltpu.VMEM((1024, 256), F32)],
        compiler_params=pltpu.CompilerParams(vmem_limit_bytes=16 * 2**20),
    )(pad(block_table), pad(grid_table))


def conv_body(flags, latent, above, below, left, right, scale, shift, weight, taps,
              ordered, depthwise, sums, conv_in, field, totals):
    lanes = weight.shape[1]
    blocks = lanes // 128

    @pl.when(pl.program_id(0) == 0)
    def _():
        turn = swapped(8, 32)
        for i in range(4):
            part = dot(turn, latent[8 * i:8 * i + 8].reshape(256, 512))
            ordered[256 * i:256 * i + 256, :] = part.astype(BF)
            conv_in[256 * i:256 * i + 256, :] = (part * scale[...] + shift[...]).astype(BF)
        start = CELLS
        for edge in (above, below, left, right):
            size = edge.shape[0]
            conv_in[start:start + size, :] = (edge[...].astype(F32) * scale[...] + shift[...]).astype(BF)
            start += size

    halo = gelu(dot(conv_in[CELLS:CELLS + HALO, :], weight[...])).astype(F32)
    place = lax.broadcasted_iota(jnp.int32, (48, 1), 0)
    corner = jnp.where(place == 32, flags[0], jnp.where(place == 33, flags[1], 1.0))
    top, bottom = halo[0:32] * flags[0], halo[32:64] * flags[1]
    west, east = halo[64:112] * (corner * flags[2]), halo[112:160] * (corner * flags[3])
    for b in range(blocks):
        cut = slice(128 * b, 128 * b + 128)
        field[b, pl.ds(48 + 7, 32, stride=48), :] = top[:, cut]
        field[b, pl.ds(48 + 40, 32, stride=48), :] = bottom[:, cut]
        for side, at in ((west, 0), (east, 33 * 48)):
            field[b, at + 8:at + 40, :] = side[0:32, cut]
            field[b, at + 7:at + 8, :] = side[32:33, cut]
            field[b, at + 40:at + 41, :] = side[33:34, cut]

    def expand(i, carry):
        rows = pl.ds(pl.multiple_of(i * 512, 512), 512)
        res = gelu(dot(conv_in[rows, :], weight[...])).astype(F32)
        for b in range(blocks):
            for t in range(2):
                for c in range(32):
                    at = 48 * (c + 1) + 8 + 16 * i + 8 * t
                    field[b, pl.ds(pl.multiple_of(at, 8), 8), :] = (
                        res[256 * t + 8 * c:256 * t + 8 * c + 8, 128 * b:128 * b + 128])
        return carry

    lax.fori_loop(0, 2, expand, 0)

    for b in range(blocks):
        cut = slice(128 * b, 128 * b + 128)
        k = [jnp.broadcast_to(taps[t:t + 1, cut], (8, 128)) for t in range(9)]

        def stencil(i, total):
            def partial(c):
                at = 48 * c + 8 + 8 * i
                up = field[b, pl.ds(at - 1, 8), :]
                mid = field[b, pl.ds(pl.multiple_of(at, 8), 8), :]
                down = field[b, pl.ds(at + 1, 8), :]
                return [k[t] * up + k[3 + t] * mid + k[6 + t] * down for t in range(3)]

            before = partial(0)
            now = partial(1)
            held = None
            for c in range(32):
                after = partial(c + 2)
                value = before[0] + now[1] + after[2]
                before, now = now, after
                if c % 2 == 0:
                    held = value
                else:
                    rows = pl.ds(pl.multiple_of(256 * i + 8 * (c - 1), 16), 16)
                    value = gelu(jnp.concatenate([held, value], axis=0))
                    depthwise[rows, cut] = value
                    wide = value.astype(F32)
                    total = total + (wide[:8] + wide[8:])
            return total

        total = lax.fori_loop(0, 4, stencil, jnp.zeros((8, 128), F32))
        totals[pl.ds(blocks * pl.program_id(0) + b, 1), :] = jnp.sum(total, axis=0, keepdims=True)

    @pl.when(pl.program_id(0) == pl.num_programs(0) - 1)
    def _():
        sums[...] = jnp.broadcast_to(totals[...].astype(BF)[None], sums.shape)


def conv_call(flags, latent, above, below, left, right, scale, shift, weight, taps, lanes=512):
    channels, wide = weight.shape
    one = lambda v: v.reshape(1, -1)
    edges = [whole(e.shape) for e in (above, below, left, right)]
    return pl.pallas_call(
        conv_body,
        grid=(wide // lanes,),
        in_specs=[pl.BlockSpec(memory_space=pltpu.SMEM), whole(latent.shape)] + edges + [
            whole((1, channels)), whole((1, channels)),
            pl.BlockSpec((channels, lanes), lambda i: (0, i)),
            pl.BlockSpec((9, lanes), lambda i: (0, i)),
        ],
        out_specs=[
            whole((CELLS, channels)),
            pl.BlockSpec((CELLS, lanes), lambda i: (0, i)),
            whole((128, wide // 128, 128)),
        ],
        out_shape=[
            jax.ShapeDtypeStruct((CELLS, channels), BF),
            jax.ShapeDtypeStruct((CELLS, wide), BF),
            jax.ShapeDtypeStruct((128, wide // 128, 128), BF),
        ],
        scratch_shapes=[
            pltpu.VMEM((CELLS + HALO, channels), BF),
            pltpu.VMEM((lanes // 128, 34 * 48, 128), F32),
            pltpu.VMEM((wide // 128, 128), F32),
        ],
        compiler_params=pltpu.CompilerParams(vmem_limit_bytes=60 * 2**20),
    )(flags, latent, above, below, left, right, one(scale), one(shift), weight, taps)


class Fetch:
    def __init__(self, sources, places, sems):
        self.copies = [pltpu.make_async_copy(s, p, sems.at[k]) for k, (s, p) in enumerate(zip(sources, places))]

    def start(self):
        for copy in self.copies:
            copy.start()

    def wait(self, *which):
        for k in which:
            self.copies[k].wait()


def attn_ff(x, wait, g1, p, pqvt, o, bias, g2, u, w, mixt, kbuf, qvt, ff_block=512):
    m, feats = x.shape
    xf = x.astype(F32)
    n = norm(xf, g1[...])
    wait(0, 1)
    kbuf[...] = dot(n, p[:, feats:2 * feats]).astype(BF)
    qvt[...] = dot_nt(pqvt[...], n).astype(BF)
    low = lax.broadcasted_iota(jnp.int32, (64, 128), 1) < 64
    zero = jnp.zeros((32, 128), BF)
    wait(2, 3)

    def pair(t, carry):
        lanes = pl.ds(pl.multiple_of(t * 128, 128), 128)
        for g in range(4):
            keys = kbuf[lanes, 128 * g:128 * g + 128]
            q = [qvt[128 * g + 32 * h:128 * g + 32 * h + 32, lanes] for h in range(4)]
            qbd = jnp.concatenate(
                [jnp.concatenate([q[h] if j == h else zero for j in range(4)], axis=0) for h in range(4)],
                axis=1)
            s4 = dot(keys, qbd)
            for h in range(4):
                head = 4 * g + h
                s = s4[:, 128 * h:128 * h + 128]
                s = jnp.where(low, s[:64], s[64:]) * (32 ** -0.5) + bias[head]
                e = jnp.exp(s - jnp.max(s, axis=0, keepdims=True))
                r = 1.0 / jnp.sum(e, axis=0, keepdims=True)
                pbd = jnp.concatenate(
                    [jnp.where(low, e, 0.0).astype(BF), jnp.where(low, 0.0, e).astype(BF)], axis=0)
                vt = qvt[512 + 32 * head:544 + 32 * head, lanes]
                mixt[32 * head:32 * head + 32, lanes] = (dot(vt, pbd) * r).astype(BF)
        return carry

    lax.fori_loop(0, m // 128, pair, 0, unroll=4)
    y = (xf + dot_tn(mixt[...], o[...])).astype(BF)
    yf = y.astype(F32)
    n2 = norm(yf, g2[...])
    acc = yf
    wait(4, 5)
    for j in range(u.shape[1] // ff_block):
        cols = slice(j * ff_block, (j + 1) * ff_block)
        hidden = gelu(dot(n2, u[:, cols]))
        acc = acc + dot(hidden, w[cols, :])
    return acc.astype(BF)


def turn_out(sec, out):
    def one(q, carry):
        for b in range(4):
            out[q, :, 128 * b:128 * b + 128] = sec[b, pl.ds(q, 16, stride=64), :].astype(BF)
        return carry

    lax.fori_loop(0, 64, one, 0, unroll=4)


def turn_in(x, sec):
    to = lax.broadcasted_iota(jnp.int32, (CELLS, CELLS), 0)
    come = lax.broadcasted_iota(jnp.int32, (CELLS, CELLS), 1)
    pick = (come == to % 64 * 16 + to // 64).astype(F32).astype(BF)
    res = dot(pick, x[...].reshape(CELLS, -1))
    for b in range(4):
        sec[b] = res[:, 128 * b:128 * b + 128]


def section_body(x, g1, g2, p_h, pqvt_h, o_h, bias_h, u_h, w_h, out,
                 p, pqvt, o, bias, u, w, mixt, kbuf, qvt, sec, sems):
    fetch = Fetch((p_h, pqvt_h, o_h, bias_h, u_h, w_h), (p, pqvt, o, bias, u, w), sems)
    fetch.start()
    turn_in(x, sec)
    m = kbuf.shape[0]

    def chunk(i, carry):
        def wait(*which):
            @pl.when(i == 0)
            def _():
                fetch.wait(*which)

        rows = pl.ds(pl.multiple_of(i * m, m), m)
        cells = jnp.concatenate([sec[b, rows, :] for b in range(4)], axis=1).astype(BF)
        res = attn_ff(cells, wait, g1, p, pqvt, o, bias, g2, u, w, mixt, kbuf, qvt).astype(F32)
        for b in range(4):
            sec[b, rows, :] = res[:, 128 * b:128 * b + 128]
        return carry

    lax.fori_loop(0, CELLS // m, chunk, 0)
    turn_out(sec, out)


def gated_body(copies, g1, g2, down_h, up_h, project_h, ordered_h, depthwise_h,
               p_h, pqvt_h, o_h, bias_h, u_h, w_h, out,
               down, up, project, ordered, depthwise, p, pqvt, o, bias, u, w,
               mixt, kbuf, qvt, sec, excite, sems):
    m = kbuf.shape[0]
    one, two = pl.ds(0, m), pl.ds(m, m)
    fetch = Fetch(
        (down_h, up_h, project_h, ordered_h, depthwise_h.at[one], p_h, pqvt_h, o_h, bias_h, u_h, w_h,
         depthwise_h.at[two]),
        (down, up, project, ordered, depthwise.at[one], p, pqvt, o, bias, u, w, depthwise.at[two]), sems)
    fetch.start()
    pooled = jnp.sum(copies[...].astype(F32), axis=0) * (1.0 / (256 * 512))
    parts = pieces(pooled)
    reduced = jnp.zeros((1, down.shape[1]), F32)
    fetch.wait(0, 1)
    for b in range(pooled.shape[0]):
        row = jnp.concatenate([part[b:b + 1, :].astype(F32) for part in parts] + [jnp.zeros((13, 128), F32)], axis=0)
        reduced = reduced + jnp.sum(dot(row.astype(BF), down[128 * b:128 * b + 128, :]), axis=0, keepdims=True)
    reduced = reduced / (1.0 + jnp.exp(-reduced))
    row = jnp.concatenate([part.astype(F32) for part in pieces(reduced)] + [jnp.zeros((13, 128), F32)], axis=0)
    raised = jnp.sum(dot(row.astype(BF), up[...]), axis=0, keepdims=True)
    excite[...] = 1.0 / (1.0 + jnp.exp(-raised))
    fetch.wait(2, 3, 4)

    def chunk(i, carry):
        def wait(*which):
            @pl.when(i == 0)
            def _():
                fetch.wait(*[5 + k for k in which])

        @pl.when(i == 1)
        def _():
            fetch.wait(11)

        rows = pl.ds(pl.multiple_of(i * m, m), m)
        acc = ordered[rows, :].astype(F32)
        for j in range(4):
            cols = slice(512 * j, 512 * j + 512)
            gated = (depthwise[rows, cols].astype(F32) * excite[:, cols]).astype(BF)
            acc = acc + dot(gated, project[cols, :])
        res = attn_ff(acc.astype(BF), wait, g1, p, pqvt, o, bias, g2, u, w, mixt, kbuf, qvt).astype(F32)
        for b in range(4):
            sec[b, rows, :] = res[:, 128 * b:128 * b + 128]
        return carry

    lax.fori_loop(0, CELLS // m, chunk, 0)
    turn_out(sec, out)


HELD = pl.BlockSpec(memory_space=pltpu.HBM)


def common_scratch(feats, m):
    return [pltpu.VMEM((feats, m), BF), pltpu.VMEM((m, feats), BF), pltpu.VMEM((2 * feats, m), BF),
            pltpu.VMEM((4, CELLS, 128), F32)]


def section_call(x, g1, g2, p, pqvt, o, bias, u, w, m=512):
    feats = x.shape[-1]
    held = (p, pqvt, o, bias, u, w)
    return pl.pallas_call(
        section_body,
        grid=(1,),
        in_specs=[whole(x.shape)] + [whole((1, feats))] * 2 + [HELD] * len(held),
        out_specs=whole((64, 16, feats)),
        out_shape=jax.ShapeDtypeStruct((64, 16, feats), BF),
        scratch_shapes=[pltpu.VMEM(a.shape, a.dtype) for a in held] + common_scratch(feats, m)
        + [pltpu.SemaphoreType.DMA((len(held),))],
        compiler_params=pltpu.CompilerParams(vmem_limit_bytes=60 * 2**20),
    )(x, g1.reshape(1, -1), g2.reshape(1, -1), *held)


def gated_call(copies, g1, g2, down, up, project, ordered, depthwise, p, pqvt, o, bias, u, w, m=512):
    feats = ordered.shape[-1]
    held = (down, up, project, ordered, depthwise, p, pqvt, o, bias, u, w)
    return pl.pallas_call(
        gated_body,
        grid=(1,),
        in_specs=[whole(copies.shape)] + [whole((1, feats))] * 2 + [HELD] * len(held),
        out_specs=whole((64, 16, feats)),
        out_shape=jax.ShapeDtypeStruct((64, 16, feats), BF),
        scratch_shapes=[pltpu.VMEM(a.shape, a.dtype) for a in held] + common_scratch(feats, m)
        + [pltpu.VMEM((1, depthwise.shape[1]), F32), pltpu.SemaphoreType.DMA((len(held) + 1,))],
        compiler_params=pltpu.CompilerParams(vmem_limit_bytes=60 * 2**20),
    )(copies, g1.reshape(1, -1), g2.reshape(1, -1), *held)


def step(cells, axis, count, forward):
    pairs = [(i, i + 1) if forward else (i + 1, i) for i in range(count - 1)]
    return lax.ppermute(cells, axis, pairs)


def per_device(
    latent, conv_scale, conv_shift, expand_weight, depth_kernel, squeeze_down, squeeze_up, project_weight,
    block_gain, block_projection, block_output, block_table, first_gain, first_expand, first_reduce,
    grid_gain, grid_projection, grid_output, grid_table, second_gain, second_expand, second_reduce,
):
    row_count, col_count, channels = latent.shape
    cols = ("ch", "core")
    above = step(latent[-1], "row", 8, True)
    below = step(latent[0], "row", 8, False)
    fill = jnp.zeros((14, channels), BF)
    left = step(jnp.concatenate([latent[:, -1], above[-1:], below[-1:], fill]), cols, 16, True)
    right = step(jnp.concatenate([latent[:, 0], above[:1], below[:1], fill]), cols, 16, False)
    row, col = lax.axis_index("row"), lax.axis_index(cols)
    flags = jnp.stack([row > 0, row < 7, col > 0, col < 15]).astype(F32)
    ordered, depthwise, copies = conv_call(
        flags, latent, above, below, left, right, conv_scale, conv_shift, expand_weight, depth_kernel
    )
    copies = lax.all_to_all(copies, ("row", "ch", "core"), 0, 0, tiled=True)

    def outer(projection):
        return jnp.concatenate([projection[:, :channels], projection[:, 2 * channels :]], axis=1).T

    def swap(windows):
        return lax.all_to_all(windows, ("row", "ch"), 0, 0, tiled=True)

    block_bias, grid_bias = bias_call(block_table, grid_table)
    windows = gated_call(
        copies, block_gain, first_gain, squeeze_down, squeeze_up, project_weight, ordered, depthwise,
        block_projection, outer(block_projection), block_output, block_bias, first_expand, first_reduce,
    )
    windows = section_call(
        swap(windows), grid_gain, second_gain,
        grid_projection, outer(grid_projection), grid_output, grid_bias, second_expand, second_reduce,
    )
    windows = swap(windows).reshape(8, 8, 4, 4, channels)
    return windows.transpose(2, 1, 3, 0, 4).reshape(row_count, col_count, channels)


def solution(mesh):
    wide = Mesh(mesh.devices.reshape(8, 8, 2), ("row", "ch", "core"))
    field = P("row", ("ch", "core"), None)
    return jax.shard_map(
        per_device, mesh=wide, in_specs=(field,) + (P(),) * 21, out_specs=field, check_vma=False
    )
```

```python
import jax
import jax.numpy as jnp
from jax import lax
from jax.experimental import pallas as pl
from jax.experimental.pallas import tpu as pltpu
from jax.sharding import Mesh, PartitionSpec as P

BF = jnp.bfloat16
F32 = jnp.float32
CELLS = 1024
HALO = 160


def norm(xf, g):
    center = xf - jnp.mean(xf, axis=-1, keepdims=True)
    spread = jnp.mean(center * center, axis=-1, keepdims=True)
    return (center * lax.rsqrt(spread + 1e-05) * g).astype(BF)


def gelu(v):
    v = v.astype(BF)
    half = v * 0.5
    return half + half * jnp.tanh(v * (v * v * 0.035677408136300125 + 0.7978845608028654))


def dot(a, b):
    return jnp.dot(a, b, preferred_element_type=F32)


def dot_nt(a, b):
    return lax.dot_general(a, b, (((1,), (1,)), ((), ())), preferred_element_type=F32)


def dot_tn(a, b):
    return lax.dot_general(a, b, (((0,), (0,)), ((), ())), preferred_element_type=F32)


def swapped(rows, cols):
    size = rows * cols
    to = lax.broadcasted_iota(jnp.int32, (size, size), 0)
    come = lax.broadcasted_iota(jnp.int32, (size, size), 1)
    return (come == (to % rows) * cols + to // rows).astype(F32).astype(BF)


def pieces(v):
    high = v.astype(BF)
    rest = v - high.astype(F32)
    mid = rest.astype(BF)
    return high, mid, (rest - mid.astype(F32)).astype(BF)


def whole(shape):
    return pl.BlockSpec(shape, lambda i: (0,) * len(shape))


def bias_body(block_tab, grid_tab, block_out, grid_out, turned):
    lane = lax.broadcasted_iota(jnp.int32, (256, 128), 1) % 64
    spot = lax.broadcasted_iota(jnp.int32, (256, 128), 0)
    for tab, out, column_major in ((block_tab, block_out, True), (grid_tab, grid_out, False)):
        slow, fast = lane // 8, lane % 8
        row, col = (fast, slow) if column_major else (slow, fast)
        pick = (spot == (row + 7) * 15 + col + 7).astype(F32).astype(BF)
        slow_step, fast_step = (1, 15) if column_major else (15, 1)
        for head in range(16):
            base = jnp.broadcast_to(tab[head:head + 1, :], (8, 256))
            for q in range(8):
                turned[64 * head + 8 * q:64 * head + 8 * q + 8, :] = pltpu.roll(
                    base, slow_step * q, 1, stride=fast_step, stride_axis=0)
        high, mid, low = pieces(turned[...])
        out[...] = (dot(high, pick) + dot(mid, pick) + dot(low, pick)).reshape(16, 64, 128)


def bias_call(block_table, grid_table):
    pad = lambda t: jnp.pad(t, ((0, 0), (0, 256 - t.shape[1])))
    shape = jax.ShapeDtypeStruct((16, 64, 128), F32)
    return pl.pallas_call(
        bias_body,
        grid=(1,),
        in_specs=[whole((16, 256))] * 2,
        out_specs=[whole((16, 64, 128))] * 2,
        out_shape=[shape, shape],
        scratch_shapes=[pltpu.VMEM((1024, 256), F32)],
        compiler_params=pltpu.CompilerParams(vmem_limit_bytes=16 * 2**20),
    )(pad(block_table), pad(grid_table))


def conv_body(flags, latent, above, below, left, right, scale, shift, weight, taps,
              ordered, depthwise, sums, conv_in, field, totals):
    lanes = weight.shape[1]
    blocks = lanes // 128

    @pl.when(pl.program_id(0) == 0)
    def _():
        turn = swapped(8, 32)
        for i in range(4):
            part = dot(turn, latent[8 * i:8 * i + 8].reshape(256, 512))
            ordered[256 * i:256 * i + 256, :] = part.astype(BF)
            conv_in[256 * i:256 * i + 256, :] = (part * scale[...] + shift[...]).astype(BF)
        start = CELLS
        for edge in (above, below, left, right):
            size = edge.shape[0]
            conv_in[start:start + size, :] = (edge[...].astype(F32) * scale[...] + shift[...]).astype(BF)
            start += size

    halo = gelu(dot(conv_in[CELLS:CELLS + HALO, :], weight[...])).astype(F32)
    place = lax.broadcasted_iota(jnp.int32, (48, 1), 0)
    corner = jnp.where(place == 32, flags[0], jnp.where(place == 33, flags[1], 1.0))
    top, bottom = halo[0:32] * flags[0], halo[32:64] * flags[1]
    west, east = halo[64:112] * (corner * flags[2]), halo[112:160] * (corner * flags[3])
    for b in range(blocks):
        cut = slice(128 * b, 128 * b + 128)
        field[b, pl.ds(48 + 7, 32, stride=48), :] = top[:, cut]
        field[b, pl.ds(48 + 40, 32, stride=48), :] = bottom[:, cut]
        for side, at in ((west, 0), (east, 33 * 48)):
            field[b, at + 8:at + 40, :] = side[0:32, cut]
            field[b, at + 7:at + 8, :] = side[32:33, cut]
            field[b, at + 40:at + 41, :] = side[33:34, cut]

    def expand(i, carry):
        rows = pl.ds(pl.multiple_of(i * 512, 512), 512)
        res = gelu(dot(conv_in[rows, :], weight[...])).astype(F32)
        for b in range(blocks):
            for t in range(2):
                for c in range(32):
                    at = 48 * (c + 1) + 8 + 16 * i + 8 * t
                    field[b, pl.ds(pl.multiple_of(at, 8), 8), :] = (
                        res[256 * t + 8 * c:256 * t + 8 * c + 8, 128 * b:128 * b + 128])
        return carry

    lax.fori_loop(0, 2, expand, 0)

    for b in range(blocks):
        cut = slice(128 * b, 128 * b + 128)
        k = [jnp.broadcast_to(taps[t:t + 1, cut], (8, 128)) for t in range(9)]

        def stencil(i, total):
            def partial(c):
                at = 48 * c + 8 + 8 * i
                up = field[b, pl.ds(at - 1, 8), :]
                mid = field[b, pl.ds(pl.multiple_of(at, 8), 8), :]
                down = field[b, pl.ds(at + 1, 8), :]
                return [k[t] * up + k[3 + t] * mid + k[6 + t] * down for t in range(3)]

            before = partial(0)
            now = partial(1)
            held = None
            for c in range(32):
                after = partial(c + 2)
                value = before[0] + now[1] + after[2]
                before, now = now, after
                if c % 2 == 0:
                    held = value
                else:
                    rows = pl.ds(pl.multiple_of(256 * i + 8 * (c - 1), 16), 16)
                    value = gelu(jnp.concatenate([held, value], axis=0))
                    depthwise[rows, cut] = value
                    wide = value.astype(F32)
                    total = total + (wide[:8] + wide[8:])
            return total

        total = lax.fori_loop(0, 4, stencil, jnp.zeros((8, 128), F32))
        totals[pl.ds(blocks * pl.program_id(0) + b, 1), :] = jnp.sum(total, axis=0, keepdims=True)

    @pl.when(pl.program_id(0) == pl.num_programs(0) - 1)
    def _():
        sums[...] = jnp.broadcast_to(totals[...].astype(BF)[None], sums.shape)


def conv_call(flags, latent, above, below, left, right, scale, shift, weight, taps, lanes=512):
    channels, wide = weight.shape
    one = lambda v: v.reshape(1, -1)
    edges = [whole(e.shape) for e in (above, below, left, right)]
    return pl.pallas_call(
        conv_body,
        grid=(wide // lanes,),
        in_specs=[pl.BlockSpec(memory_space=pltpu.SMEM), whole(latent.shape)] + edges + [
            whole((1, channels)), whole((1, channels)),
            pl.BlockSpec((channels, lanes), lambda i: (0, i)),
            pl.BlockSpec((9, lanes), lambda i: (0, i)),
        ],
        out_specs=[
            whole((CELLS, channels)),
            pl.BlockSpec((CELLS, lanes), lambda i: (0, i)),
            whole((128, wide // 128, 128)),
        ],
        out_shape=[
            jax.ShapeDtypeStruct((CELLS, channels), BF),
            jax.ShapeDtypeStruct((CELLS, wide), BF),
            jax.ShapeDtypeStruct((128, wide // 128, 128), BF),
        ],
        scratch_shapes=[
            pltpu.VMEM((CELLS + HALO, channels), BF),
            pltpu.VMEM((lanes // 128, 34 * 48, 128), F32),
            pltpu.VMEM((wide // 128, 128), F32),
        ],
        compiler_params=pltpu.CompilerParams(vmem_limit_bytes=60 * 2**20),
    )(flags, latent, above, below, left, right, one(scale), one(shift), weight, taps)


class Fetch:
    def __init__(self, sources, places, sems):
        self.copies = [pltpu.make_async_copy(s, p, sems.at[k]) for k, (s, p) in enumerate(zip(sources, places))]

    def start(self, *which):
        for k in which:
            self.copies[k].start()

    def wait(self, *which):
        for k in which:
            self.copies[k].wait()


def attn_ff(x, wait, g1, p, pqvt, o, bias, g2, u, w, mixt, kbuf, qvt, ff_block=512):
    m, feats = x.shape
    xf = x.astype(F32)
    n = norm(xf, g1[...])
    wait(0, 1)
    kbuf[...] = dot(n, p[:, feats:2 * feats]).astype(BF)
    qvt[...] = dot_nt(pqvt[...], n).astype(BF)
    low = lax.broadcasted_iota(jnp.int32, (64, 128), 1) < 64
    zero = jnp.zeros((32, 128), BF)
    wait(2, 3)

    def pair(t, carry):
        lanes = pl.ds(pl.multiple_of(t * 128, 128), 128)
        for g in range(4):
            keys = kbuf[lanes, 128 * g:128 * g + 128]
            q = [qvt[128 * g + 32 * h:128 * g + 32 * h + 32, lanes] for h in range(4)]
            qbd = jnp.concatenate(
                [jnp.concatenate([q[h] if j == h else zero for j in range(4)], axis=0) for h in range(4)],
                axis=1)
            s4 = dot(keys, qbd)
            for h in range(4):
                head = 4 * g + h
                s = s4[:, 128 * h:128 * h + 128]
                s = jnp.where(low, s[:64], s[64:]) * (32 ** -0.5) + bias[head]
                e = jnp.exp(s - jnp.max(s, axis=0, keepdims=True))
                r = 1.0 / jnp.sum(e, axis=0, keepdims=True)
                pbd = jnp.concatenate(
                    [jnp.where(low, e, 0.0).astype(BF), jnp.where(low, 0.0, e).astype(BF)], axis=0)
                vt = qvt[512 + 32 * head:544 + 32 * head, lanes]
                mixt[32 * head:32 * head + 32, lanes] = (dot(vt, pbd) * r).astype(BF)
        return carry

    lax.fori_loop(0, m // 128, pair, 0, unroll=4)
    y = (xf + dot_tn(mixt[...], o[...])).astype(BF)
    yf = y.astype(F32)
    n2 = norm(yf, g2[...])
    acc = yf
    wait(4, 5)
    for j in range(u.shape[1] // ff_block):
        cols = slice(j * ff_block, (j + 1) * ff_block)
        hidden = gelu(dot(n2, u[:, cols]))
        acc = acc + dot(hidden, w[cols, :])
    return acc.astype(BF)


PITCH = 72


def put(sec, first, res):
    for b in range(4):
        for t in range(res.shape[0] // 64):
            rows = pl.ds(pl.multiple_of((first + t) * PITCH, 8), 64)
            sec[b, rows, :] = res[64 * t:64 * t + 64, 128 * b:128 * b + 128]


def turn_out(sec, out):
    def one(q, carry):
        for b in range(4):
            out[q, :, 128 * b:128 * b + 128] = sec[b, pl.ds(q, 16, stride=PITCH), :].astype(BF)
        return carry

    lax.fori_loop(0, 64, one, 0, unroll=4)


def turn_in(x, sec, wait):
    to = lax.broadcasted_iota(jnp.int32, (CELLS, CELLS), 0)
    come = lax.broadcasted_iota(jnp.int32, (CELLS, CELLS), 1)
    pick = (come == to % 64 * 16 + to // 64).astype(F32).astype(BF)
    wait(6)
    res = dot(pick, x[...].reshape(CELLS, -1))
    put(sec, 0, res)


def section_body(x_h, g1, g2, p_h, pqvt_h, o_h, bias_h, u_h, w_h, out,
                 x, p, pqvt, o, bias, u, w, mixt, kbuf, qvt, sec, sems):
    fetch = Fetch((p_h, pqvt_h, o_h, bias_h, u_h, w_h, x_h), (p, pqvt, o, bias, u, w, x), sems)
    fetch.start(6, 0, 1)
    turn_in(x, sec, fetch.wait)
    m = kbuf.shape[0]

    def chunk(i, carry):
        def wait(*which):
            @pl.when(i == 0)
            def _():
                fetch.wait(*which)
                if 1 in which:
                    fetch.start(2, 3, 4, 5)

        cells = jnp.concatenate(
            [jnp.concatenate(
                [sec[b, pl.ds(pl.multiple_of((i * (m // 64) + t) * PITCH, 8), 64), :] for t in range(m // 64)], axis=0)
             for b in range(4)], axis=1).astype(BF)
        res = attn_ff(cells, wait, g1, p, pqvt, o, bias, g2, u, w, mixt, kbuf, qvt).astype(F32)
        put(sec, i * (m // 64), res)
        return carry

    lax.fori_loop(0, CELLS // m, chunk, 0)
    turn_out(sec, out)


def gated_body(copies_h, g1, g2, down_h, up_h, project_h, ordered_h, depthwise_h,
               p_h, pqvt_h, o_h, bias_h, u_h, w_h, out,
               copies, down, up, project, ordered, depthwise, p, pqvt, o, bias, u, w,
               mixt, kbuf, qvt, sec, excite, sems):
    m = kbuf.shape[0]
    one, two = pl.ds(0, m), pl.ds(m, m)
    fetch = Fetch(
        (copies_h, down_h, up_h, project_h, ordered_h, depthwise_h.at[one], p_h, pqvt_h, o_h, bias_h, u_h, w_h,
         depthwise_h.at[two]),
        (copies, down, up, project, ordered, depthwise.at[one], p, pqvt, o, bias, u, w, depthwise.at[two]), sems)
    fetch.start(0, 1, 2, 3, 4, 5)
    fetch.wait(0)
    pooled = jnp.sum(copies[...].astype(F32), axis=0) * (1.0 / (256 * 512))
    parts = pieces(pooled)
    reduced = jnp.zeros((1, down.shape[1]), F32)
    fetch.wait(1, 2)
    for b in range(pooled.shape[0]):
        row = jnp.concatenate([part[b:b + 1, :].astype(F32) for part in parts] + [jnp.zeros((13, 128), F32)], axis=0)
        reduced = reduced + jnp.sum(dot(row.astype(BF), down[128 * b:128 * b + 128, :]), axis=0, keepdims=True)
    reduced = reduced / (1.0 + jnp.exp(-reduced))
    row = jnp.concatenate([part.astype(F32) for part in pieces(reduced)] + [jnp.zeros((13, 128), F32)], axis=0)
    raised = jnp.sum(dot(row.astype(BF), up[...]), axis=0, keepdims=True)
    excite[...] = 1.0 / (1.0 + jnp.exp(-raised))
    fetch.wait(3, 4, 5)
    fetch.start(6, 7)

    def chunk(i, carry):
        def wait(*which):
            @pl.when(i == 0)
            def _():
                fetch.wait(*[6 + k for k in which])
                if 1 in which:
                    fetch.start(8, 9, 10, 11, 12)

        @pl.when(i == 1)
        def _():
            fetch.wait(12)

        rows = pl.ds(pl.multiple_of(i * m, m), m)
        acc = ordered[rows, :].astype(F32)
        for j in range(4):
            cols = slice(512 * j, 512 * j + 512)
            gated = (depthwise[rows, cols].astype(F32) * excite[:, cols]).astype(BF)
            acc = acc + dot(gated, project[cols, :])
        res = attn_ff(acc.astype(BF), wait, g1, p, pqvt, o, bias, g2, u, w, mixt, kbuf, qvt).astype(F32)
        put(sec, i * (m // 64), res)
        return carry

    lax.fori_loop(0, CELLS // m, chunk, 0)
    turn_out(sec, out)


HELD = pl.BlockSpec(memory_space=pltpu.HBM)


def common_scratch(feats, m):
    return [pltpu.VMEM((feats, m), BF), pltpu.VMEM((m, feats), BF), pltpu.VMEM((2 * feats, m), BF),
            pltpu.VMEM((4, 16 * PITCH, 128), F32)]


def section_call(x, g1, g2, p, pqvt, o, bias, u, w, m=512):
    feats = x.shape[-1]
    held = (p, pqvt, o, bias, u, w)
    return pl.pallas_call(
        section_body,
        grid=(1,),
        in_specs=[HELD] + [whole((1, feats))] * 2 + [HELD] * len(held),
        out_specs=whole((64, 16, feats)),
        out_shape=jax.ShapeDtypeStruct((64, 16, feats), BF),
        scratch_shapes=[pltpu.VMEM(a.shape, a.dtype) for a in (x,) + held] + common_scratch(feats, m)
        + [pltpu.SemaphoreType.DMA((len(held) + 1,))],
        compiler_params=pltpu.CompilerParams(vmem_limit_bytes=60 * 2**20),
    )(x, g1.reshape(1, -1), g2.reshape(1, -1), *held)


def gated_call(copies, g1, g2, down, up, project, ordered, depthwise, p, pqvt, o, bias, u, w, m=512):
    feats = ordered.shape[-1]
    held = (down, up, project, ordered, depthwise, p, pqvt, o, bias, u, w)
    return pl.pallas_call(
        gated_body,
        grid=(1,),
        in_specs=[HELD] + [whole((1, feats))] * 2 + [HELD] * len(held),
        out_specs=whole((64, 16, feats)),
        out_shape=jax.ShapeDtypeStruct((64, 16, feats), BF),
        scratch_shapes=[pltpu.VMEM(a.shape, a.dtype) for a in (copies,) + held] + common_scratch(feats, m)
        + [pltpu.VMEM((1, depthwise.shape[1]), F32), pltpu.SemaphoreType.DMA((len(held) + 2,))],
        compiler_params=pltpu.CompilerParams(vmem_limit_bytes=60 * 2**20),
    )(copies, g1.reshape(1, -1), g2.reshape(1, -1), *held)


def step(cells, axis, count, forward):
    pairs = [(i, i + 1) if forward else (i + 1, i) for i in range(count - 1)]
    return lax.ppermute(cells, axis, pairs)


def per_device(
    latent, conv_scale, conv_shift, expand_weight, depth_kernel, squeeze_down, squeeze_up, project_weight,
    block_gain, block_projection, block_output, block_table, first_gain, first_expand, first_reduce,
    grid_gain, grid_projection, grid_output, grid_table, second_gain, second_expand, second_reduce,
):
    row_count, col_count, channels = latent.shape
    cols = ("ch", "core")
    above = step(latent[-1], "row", 8, True)
    below = step(latent[0], "row", 8, False)
    fill = jnp.zeros((14, channels), BF)
    left = step(jnp.concatenate([latent[:, -1], above[-1:], below[-1:], fill]), cols, 16, True)
    right = step(jnp.concatenate([latent[:, 0], above[:1], below[:1], fill]), cols, 16, False)
    row, col = lax.axis_index("row"), lax.axis_index(cols)
    flags = jnp.stack([row > 0, row < 7, col > 0, col < 15]).astype(F32)
    ordered, depthwise, copies = conv_call(
        flags, latent, above, below, left, right, conv_scale, conv_shift, expand_weight, depth_kernel
    )
    copies = lax.all_to_all(copies, ("row", "ch", "core"), 0, 0, tiled=True)

    def outer(projection):
        return jnp.concatenate([projection[:, :channels], projection[:, 2 * channels :]], axis=1).T

    def swap(windows):
        return lax.all_to_all(windows, ("row", "ch"), 0, 0, tiled=True)

    block_bias, grid_bias = bias_call(block_table, grid_table)
    windows = gated_call(
        copies, block_gain, first_gain, squeeze_down, squeeze_up, project_weight, ordered, depthwise,
        block_projection, outer(block_projection), block_output, block_bias, first_expand, first_reduce,
    )
    windows = section_call(
        swap(windows), grid_gain, second_gain,
        grid_projection, outer(grid_projection), grid_output, grid_bias, second_expand, second_reduce, m=1024,
    )
    windows = swap(windows).reshape(8, 8, 4, 4, channels)
    return windows.transpose(2, 1, 3, 0, 4).reshape(row_count, col_count, channels)


def solution(mesh):
    wide = Mesh(mesh.devices.reshape(8, 8, 2), ("row", "ch", "core"))
    field = P("row", ("ch", "core"), None)
    return jax.shard_map(
        per_device, mesh=wide, in_specs=(field,) + (P(),) * 21, out_specs=field, check_vma=False
    )
```

```python
import jax
import jax.numpy as jnp
from jax import lax
from jax.experimental import pallas as pl
from jax.experimental.pallas import tpu as pltpu
from jax.sharding import Mesh, PartitionSpec as P

BF = jnp.bfloat16
F32 = jnp.float32
CELLS = 1024
HALO = 160


def norm(xf, g):
    center = xf - jnp.mean(xf, axis=-1, keepdims=True)
    spread = jnp.mean(center * center, axis=-1, keepdims=True)
    return (center * lax.rsqrt(spread + 1e-05) * g).astype(BF)


def gelu(v):
    v = v.astype(BF)
    half = v * 0.5
    return half + half * jnp.tanh(v * (v * v * 0.035677408136300125 + 0.7978845608028654))


def dot(a, b):
    return jnp.dot(a, b, preferred_element_type=F32)


def dot_nt(a, b):
    return lax.dot_general(a, b, (((1,), (1,)), ((), ())), preferred_element_type=F32)


def dot_tn(a, b):
    return lax.dot_general(a, b, (((0,), (0,)), ((), ())), preferred_element_type=F32)


def swapped(rows, cols):
    size = rows * cols
    to = lax.broadcasted_iota(jnp.int32, (size, size), 0)
    come = lax.broadcasted_iota(jnp.int32, (size, size), 1)
    return (come == (to % rows) * cols + to // rows).astype(F32).astype(BF)


def pieces(v):
    high = v.astype(BF)
    rest = v - high.astype(F32)
    mid = rest.astype(BF)
    return high, mid, (rest - mid.astype(F32)).astype(BF)


def whole(shape):
    return pl.BlockSpec(shape, lambda i: (0,) * len(shape))


def bias_body(block_tab, grid_tab, block_out, grid_out, turned):
    lane = lax.broadcasted_iota(jnp.int32, (256, 128), 1) % 64
    spot = lax.broadcasted_iota(jnp.int32, (256, 128), 0)
    for tab, out, column_major in ((block_tab, block_out, True), (grid_tab, grid_out, False)):
        slow, fast = lane // 8, lane % 8
        row, col = (fast, slow) if column_major else (slow, fast)
        pick = (spot == (row + 7) * 15 + col + 7).astype(F32).astype(BF)
        slow_step, fast_step = (1, 15) if column_major else (15, 1)
        for head in range(16):
            base = jnp.broadcast_to(tab[head:head + 1, :], (8, 256))
            for q in range(8):
                turned[64 * head + 8 * q:64 * head + 8 * q + 8, :] = pltpu.roll(
                    base, slow_step * q, 1, stride=fast_step, stride_axis=0)
        high, mid, low = pieces(turned[...])
        out[...] = (dot(high, pick) + dot(mid, pick) + dot(low, pick)).reshape(16, 64, 128)


def bias_call(block_table, grid_table):
    pad = lambda t: jnp.pad(t, ((0, 0), (0, 256 - t.shape[1])))
    shape = jax.ShapeDtypeStruct((16, 64, 128), F32)
    return pl.pallas_call(
        bias_body,
        grid=(1,),
        in_specs=[whole((16, 256))] * 2,
        out_specs=[whole((16, 64, 128))] * 2,
        out_shape=[shape, shape],
        scratch_shapes=[pltpu.VMEM((1024, 256), F32)],
        compiler_params=pltpu.CompilerParams(vmem_limit_bytes=16 * 2**20),
    )(pad(block_table), pad(grid_table))


def conv_body(flags, latent, above, below, left, right, scale, shift, weight, taps,
              ordered, depthwise, sums, conv_in, field, totals):
    lanes = weight.shape[1]
    blocks = lanes // 128

    @pl.when(pl.program_id(0) == 0)
    def _():
        turn = swapped(8, 32)
        for i in range(4):
            part = dot(turn, latent[8 * i:8 * i + 8].reshape(256, 512))
            ordered[256 * i:256 * i + 256, :] = part.astype(BF)
            conv_in[256 * i:256 * i + 256, :] = (part * scale[...] + shift[...]).astype(BF)
        start = CELLS
        for edge in (above, below, left, right):
            size = edge.shape[0]
            conv_in[start:start + size, :] = (edge[...].astype(F32) * scale[...] + shift[...]).astype(BF)
            start += size

    halo = gelu(dot(conv_in[CELLS:CELLS + HALO, :], weight[...])).astype(F32)
    place = lax.broadcasted_iota(jnp.int32, (48, 1), 0)
    corner = jnp.where(place == 32, flags[0], jnp.where(place == 33, flags[1], 1.0))
    top, bottom = halo[0:32] * flags[0], halo[32:64] * flags[1]
    west, east = halo[64:112] * (corner * flags[2]), halo[112:160] * (corner * flags[3])
    for b in range(blocks):
        cut = slice(128 * b, 128 * b + 128)
        field[b, pl.ds(48 + 7, 32, stride=48), :] = top[:, cut]
        field[b, pl.ds(48 + 40, 32, stride=48), :] = bottom[:, cut]
        for side, at in ((west, 0), (east, 33 * 48)):
            field[b, at + 8:at + 40, :] = side[0:32, cut]
            field[b, at + 7:at + 8, :] = side[32:33, cut]
            field[b, at + 40:at + 41, :] = side[33:34, cut]

    def expand(i, carry):
        rows = pl.ds(pl.multiple_of(i * 512, 512), 512)
        res = gelu(dot(conv_in[rows, :], weight[...])).astype(F32)
        for b in range(blocks):
            for t in range(2):
                for c in range(32):
                    at = 48 * (c + 1) + 8 + 16 * i + 8 * t
                    field[b, pl.ds(pl.multiple_of(at, 8), 8), :] = (
                        res[256 * t + 8 * c:256 * t + 8 * c + 8, 128 * b:128 * b + 128])
        return carry

    lax.fori_loop(0, 2, expand, 0)

    for b in range(blocks):
        cut = slice(128 * b, 128 * b + 128)
        k = [jnp.broadcast_to(taps[t:t + 1, cut], (8, 128)) for t in range(9)]

        def stencil(i, total):
            def partial(c):
                at = 48 * c + 8 + 8 * i
                up = field[b, pl.ds(at - 1, 8), :]
                mid = field[b, pl.ds(pl.multiple_of(at, 8), 8), :]
                down = field[b, pl.ds(at + 1, 8), :]
                return [k[t] * up + k[3 + t] * mid + k[6 + t] * down for t in range(3)]

            before = partial(0)
            now = partial(1)
            held = None
            for c in range(32):
                after = partial(c + 2)
                value = before[0] + now[1] + after[2]
                before, now = now, after
                if c % 2 == 0:
                    held = value
                else:
                    rows = pl.ds(pl.multiple_of(256 * i + 8 * (c - 1), 16), 16)
                    value = gelu(jnp.concatenate([held, value], axis=0))
                    depthwise[rows, cut] = value
                    wide = value.astype(F32)
                    total = total + (wide[:8] + wide[8:])
            return total

        total = lax.fori_loop(0, 4, stencil, jnp.zeros((8, 128), F32))
        totals[pl.ds(blocks * pl.program_id(0) + b, 1), :] = jnp.sum(total, axis=0, keepdims=True)

    @pl.when(pl.program_id(0) == pl.num_programs(0) - 1)
    def _():
        sums[...] = jnp.broadcast_to(totals[...].astype(BF)[None], sums.shape)


def conv_call(flags, latent, above, below, left, right, scale, shift, weight, taps, lanes=512):
    channels, wide = weight.shape
    one = lambda v: v.reshape(1, -1)
    edges = [whole(e.shape) for e in (above, below, left, right)]
    return pl.pallas_call(
        conv_body,
        grid=(wide // lanes,),
        in_specs=[pl.BlockSpec(memory_space=pltpu.SMEM), whole(latent.shape)] + edges + [
            whole((1, channels)), whole((1, channels)),
            pl.BlockSpec((channels, lanes), lambda i: (0, i)),
            pl.BlockSpec((9, lanes), lambda i: (0, i)),
        ],
        out_specs=[
            whole((CELLS, channels)),
            pl.BlockSpec((CELLS, lanes), lambda i: (0, i)),
            whole((128, wide // 128, 128)),
        ],
        out_shape=[
            jax.ShapeDtypeStruct((CELLS, channels), BF),
            jax.ShapeDtypeStruct((CELLS, wide), BF),
            jax.ShapeDtypeStruct((128, wide // 128, 128), BF),
        ],
        scratch_shapes=[
            pltpu.VMEM((CELLS + HALO, channels), BF),
            pltpu.VMEM((lanes // 128, 34 * 48, 128), F32),
            pltpu.VMEM((wide // 128, 128), F32),
        ],
        compiler_params=pltpu.CompilerParams(vmem_limit_bytes=60 * 2**20),
    )(flags, latent, above, below, left, right, one(scale), one(shift), weight, taps)


class Fetch:
    def __init__(self, sources, places, sems):
        self.copies = [pltpu.make_async_copy(s, p, sems.at[k]) for k, (s, p) in enumerate(zip(sources, places))]

    def start(self, *which):
        for k in which:
            self.copies[k].start()

    def wait(self, *which):
        for k in which:
            self.copies[k].wait()


def attn_ff(x, wait, g1, p, pqvt, o, bias, g2, u, w, mixt, kbuf, qvt, ff_block=512):
    m, feats = x.shape
    xf = x.astype(F32)
    n = norm(xf, g1[...])
    wait(0, 1)
    kbuf[...] = dot(n, p[:, feats:2 * feats]).astype(BF)
    qvt[...] = dot_nt(pqvt[...], n).astype(BF)
    low = lax.broadcasted_iota(jnp.int32, (64, 128), 1) < 64
    zero = jnp.zeros((32, 128), BF)
    wait(2, 3)

    def pair(t, carry):
        lanes = pl.ds(pl.multiple_of(t * 128, 128), 128)
        for g in range(4):
            keys = kbuf[lanes, 128 * g:128 * g + 128]
            q = [qvt[128 * g + 32 * h:128 * g + 32 * h + 32, lanes] for h in range(4)]
            qbd = jnp.concatenate(
                [jnp.concatenate([q[h] if j == h else zero for j in range(4)], axis=0) for h in range(4)],
                axis=1)
            s4 = dot(keys, qbd)
            for h in range(4):
                head = 4 * g + h
                s = s4[:, 128 * h:128 * h + 128]
                s = jnp.where(low, s[:64], s[64:]) * (32 ** -0.5) + bias[head]
                e = jnp.exp(s - jnp.max(s, axis=0, keepdims=True))
                r = 1.0 / jnp.sum(e, axis=0, keepdims=True)
                pbd = jnp.concatenate(
                    [jnp.where(low, e, 0.0).astype(BF), jnp.where(low, 0.0, e).astype(BF)], axis=0)
                vt = qvt[512 + 32 * head:544 + 32 * head, lanes]
                mixt[32 * head:32 * head + 32, lanes] = (dot(vt, pbd) * r).astype(BF)
        return carry

    lax.fori_loop(0, m // 128, pair, 0, unroll=4)
    y = (xf + dot_tn(mixt[...], o[...])).astype(BF)
    yf = y.astype(F32)
    n2 = norm(yf, g2[...])
    acc = yf
    wait(4, 5)
    for j in range(u.shape[1] // ff_block):
        cols = slice(j * ff_block, (j + 1) * ff_block)
        hidden = gelu(dot(n2, u[:, cols]))
        acc = acc + dot(hidden, w[cols, :])
    return acc.astype(BF)


PITCH = 72


def put(sec, first, res):
    for b in range(4):
        for t in range(res.shape[0] // 64):
            rows = pl.ds(pl.multiple_of((first + t) * PITCH, 8), 64)
            sec[b, rows, :] = res[64 * t:64 * t + 64, 128 * b:128 * b + 128]


def turn_out(sec, out):
    def one(q, carry):
        for b in range(4):
            out[q, :, 128 * b:128 * b + 128] = sec[b, pl.ds(q, 16, stride=PITCH), :].astype(BF)
        return carry

    lax.fori_loop(0, 64, one, 0, unroll=4)


def turn_in(x, sec, wait):
    to = lax.broadcasted_iota(jnp.int32, (CELLS, CELLS), 0)
    come = lax.broadcasted_iota(jnp.int32, (CELLS, CELLS), 1)
    pick = (come == to % 64 * 16 + to // 64).astype(F32).astype(BF)
    wait(6)
    res = dot(pick, x[...].reshape(CELLS, -1))
    put(sec, 0, res)


def section_body(x_h, g1, g2, p_h, pqvt_h, o_h, bias_h, u_h, w_h, out,
                 x, p, pqvt, o, bias, u, w, mixt, kbuf, qvt, sec, sems):
    fetch = Fetch((p_h, pqvt_h, o_h, bias_h, u_h, w_h, x_h), (p, pqvt, o, bias, u, w, x), sems)
    fetch.start(6, 0, 1)
    turn_in(x, sec, fetch.wait)
    m = kbuf.shape[0]

    def chunk(i, carry):
        def wait(*which):
            @pl.when(i == 0)
            def _():
                fetch.wait(*which)
                if 1 in which:
                    fetch.start(2, 3, 4, 5)

        cells = jnp.concatenate(
            [jnp.concatenate(
                [sec[b, pl.ds(pl.multiple_of((i * (m // 64) + t) * PITCH, 8), 64), :] for t in range(m // 64)], axis=0)
             for b in range(4)], axis=1).astype(BF)
        res = attn_ff(cells, wait, g1, p, pqvt, o, bias, g2, u, w, mixt, kbuf, qvt).astype(F32)
        put(sec, i * (m // 64), res)
        return carry

    lax.fori_loop(0, CELLS // m, chunk, 0)
    turn_out(sec, out)


def gated_body(copies_h, g1, g2, down_h, up_h, project_h, ordered_h, depthwise_h,
               p_h, pqvt_h, o_h, bias_h, u_h, w_h, out,
               copies, down, up, project, ordered, depthwise, p, pqvt, o, bias, u, w,
               mixt, kbuf, qvt, sec, excite, sems):
    m = kbuf.shape[0]
    one, two = pl.ds(0, m), pl.ds(m, m)
    fetch = Fetch(
        (copies_h, down_h, up_h, project_h, ordered_h, depthwise_h.at[one], p_h, pqvt_h, o_h, bias_h, u_h, w_h,
         depthwise_h.at[two]),
        (copies, down, up, project, ordered, depthwise.at[one], p, pqvt, o, bias, u, w, depthwise.at[two]), sems)
    fetch.start(0, 1, 2, 3, 4, 5)
    fetch.wait(0)
    pooled = jnp.sum(copies[...].astype(F32), axis=0) * (1.0 / (256 * 512))
    parts = pieces(pooled)
    reduced = jnp.zeros((1, down.shape[1]), F32)
    fetch.wait(1, 2)
    for b in range(pooled.shape[0]):
        row = jnp.concatenate([part[b:b + 1, :].astype(F32) for part in parts] + [jnp.zeros((13, 128), F32)], axis=0)
        reduced = reduced + jnp.sum(dot(row.astype(BF), down[128 * b:128 * b + 128, :]), axis=0, keepdims=True)
    reduced = reduced / (1.0 + jnp.exp(-reduced))
    row = jnp.concatenate([part.astype(F32) for part in pieces(reduced)] + [jnp.zeros((13, 128), F32)], axis=0)
    raised = jnp.sum(dot(row.astype(BF), up[...]), axis=0, keepdims=True)
    excite[...] = 1.0 / (1.0 + jnp.exp(-raised))
    fetch.wait(3, 4, 5)
    fetch.start(6, 7)

    def chunk(i, carry):
        def wait(*which):
            @pl.when(i == 0)
            def _():
                fetch.wait(*[6 + k for k in which])
                if 1 in which:
                    fetch.start(8, 9, 10, 11, 12)

        @pl.when(i == 1)
        def _():
            fetch.wait(12)

        rows = pl.ds(pl.multiple_of(i * m, m), m)
        acc = ordered[rows, :].astype(F32)
        for j in range(4):
            cols = slice(512 * j, 512 * j + 512)
            gated = depthwise[rows, cols] * excite[:, cols].astype(BF)
            acc = acc + dot(gated, project[cols, :])
        res = attn_ff(acc.astype(BF), wait, g1, p, pqvt, o, bias, g2, u, w, mixt, kbuf, qvt).astype(F32)
        put(sec, i * (m // 64), res)
        return carry

    lax.fori_loop(0, CELLS // m, chunk, 0)
    turn_out(sec, out)


HELD = pl.BlockSpec(memory_space=pltpu.HBM)


def common_scratch(feats, m):
    return [pltpu.VMEM((feats, m), BF), pltpu.VMEM((m, feats), BF), pltpu.VMEM((2 * feats, m), BF),
            pltpu.VMEM((4, 16 * PITCH, 128), F32)]


def section_call(x, g1, g2, p, pqvt, o, bias, u, w, m=512):
    feats = x.shape[-1]
    held = (p, pqvt, o, bias, u, w)
    return pl.pallas_call(
        section_body,
        grid=(1,),
        in_specs=[HELD] + [whole((1, feats))] * 2 + [HELD] * len(held),
        out_specs=whole((64, 16, feats)),
        out_shape=jax.ShapeDtypeStruct((64, 16, feats), BF),
        scratch_shapes=[pltpu.VMEM(a.shape, a.dtype) for a in (x,) + held] + common_scratch(feats, m)
        + [pltpu.SemaphoreType.DMA((len(held) + 1,))],
        compiler_params=pltpu.CompilerParams(vmem_limit_bytes=60 * 2**20),
    )(x, g1.reshape(1, -1), g2.reshape(1, -1), *held)


def gated_call(copies, g1, g2, down, up, project, ordered, depthwise, p, pqvt, o, bias, u, w, m=512):
    feats = ordered.shape[-1]
    held = (down, up, project, ordered, depthwise, p, pqvt, o, bias, u, w)
    return pl.pallas_call(
        gated_body,
        grid=(1,),
        in_specs=[HELD] + [whole((1, feats))] * 2 + [HELD] * len(held),
        out_specs=whole((64, 16, feats)),
        out_shape=jax.ShapeDtypeStruct((64, 16, feats), BF),
        scratch_shapes=[pltpu.VMEM(a.shape, a.dtype) for a in (copies,) + held] + common_scratch(feats, m)
        + [pltpu.VMEM((1, depthwise.shape[1]), F32), pltpu.SemaphoreType.DMA((len(held) + 2,))],
        compiler_params=pltpu.CompilerParams(vmem_limit_bytes=60 * 2**20),
    )(copies, g1.reshape(1, -1), g2.reshape(1, -1), *held)


def step(cells, axis, count, forward):
    pairs = [(i, i + 1) if forward else (i + 1, i) for i in range(count - 1)]
    return lax.ppermute(cells, axis, pairs)


def per_device(
    latent, conv_scale, conv_shift, expand_weight, depth_kernel, squeeze_down, squeeze_up, project_weight,
    block_gain, block_projection, block_output, block_table, first_gain, first_expand, first_reduce,
    grid_gain, grid_projection, grid_output, grid_table, second_gain, second_expand, second_reduce,
):
    row_count, col_count, channels = latent.shape
    cols = ("ch", "core")
    above = step(latent[-1], "row", 8, True)
    below = step(latent[0], "row", 8, False)
    fill = jnp.zeros((14, channels), BF)
    left = step(jnp.concatenate([latent[:, -1], above[-1:], below[-1:], fill]), cols, 16, True)
    right = step(jnp.concatenate([latent[:, 0], above[:1], below[:1], fill]), cols, 16, False)
    row, col = lax.axis_index("row"), lax.axis_index(cols)
    flags = jnp.stack([row > 0, row < 7, col > 0, col < 15]).astype(F32)
    ordered, depthwise, copies = conv_call(
        flags, latent, above, below, left, right, conv_scale, conv_shift, expand_weight, depth_kernel
    )
    copies = lax.all_to_all(copies, ("row", "ch", "core"), 0, 0, tiled=True)

    def outer(projection):
        return jnp.concatenate([projection[:, :channels], projection[:, 2 * channels :]], axis=1).T

    def swap(windows):
        return lax.all_to_all(windows, ("row", "ch"), 0, 0, tiled=True)

    block_bias, grid_bias = bias_call(block_table, grid_table)
    windows = gated_call(
        copies, block_gain, first_gain, squeeze_down, squeeze_up, project_weight, ordered, depthwise,
        block_projection, outer(block_projection), block_output, block_bias, first_expand, first_reduce,
    )
    windows = section_call(
        swap(windows), grid_gain, second_gain,
        grid_projection, outer(grid_projection), grid_output, grid_bias, second_expand, second_reduce, m=1024,
    )
    windows = swap(windows).reshape(8, 8, 4, 4, channels)
    return windows.transpose(2, 1, 3, 0, 4).reshape(row_count, col_count, channels)


def solution(mesh):
    wide = Mesh(mesh.devices.reshape(8, 8, 2), ("row", "ch", "core"))
    field = P("row", ("ch", "core"), None)
    return jax.shard_map(
        per_device, mesh=wide, in_specs=(field,) + (P(),) * 21, out_specs=field, check_vma=False
    )
```
